256 devices in a mesh: slab: 64 (over z, x, core), tile: 4 (over y).
Axes of the slice: x: 4, y: 4, z: 8, core: 2. Of those that a mesh axis runs over, the one named last changes fastest.
Arguments:
- volume: float32 [1024, 256, 512], P('slab', 'tile'), may hold values from -6 to 6
- knot_bins: int32 [8], replicated, may hold values from 0 to 255, as said below
- colour_table: float32 [4, 8], replicated, may hold values from 0.001 to 1
- view_side: int32 [512], replicated, may hold values from 0 to 1
Outputs:
- image: float32 [4, 64, 4, 512], P(None, 'slab', 'tile')
The draws below stay inside these ranges and needn't reach their ends.
Inputs may be any that keep to these rules, and one draw needn't show every extreme that they name: `knot_bins`: strictly increasing; the first is 0 and the last is 255.
All inputs are finite; a program needn't handle non-finite values.
Results may differ from the reference program's by a relative error of at most 0.0003.
Values sent between devices are 32-bit elements; how exact they have to be, the bound alone decides.
No kernel may reach another device: no remote copies, remote signals or barrier semaphores. Data moves between devices by JAX's collectives and lax.ppermute only.
A program may use at most 64 MiB of HBM per device.

```python
import jax
import jax.numpy as jnp
from jax import lax

NX = 512
BINS = 256
KNOTS = 8
NZ = 1024
NY = 256
RB = 1
N_SLAB = 64
N_TILE = 4


def draw_knot_bins(key, part):
    key = jax.random.fold_in(key, 11)
    key_low, key_high, key_mid = jax.random.split(key, 3)
    second = jax.random.randint(key_low, (1,), 12, 29).astype(jnp.int32)
    before_last = jax.random.randint(key_high, (1,), 227, 244).astype(jnp.int32)
    middle = jax.random.permutation(key_mid, 198)[:KNOTS - 4] + 29
    middle = jnp.sort(middle).astype(jnp.int32)
    first = jnp.zeros((1,), jnp.int32)
    final_bin = jnp.full((1,), BINS - 1, jnp.int32)
    return jnp.concatenate([first, second, middle, before_last, final_bin])


def draw_colour_table(key, part):
    key = jax.random.fold_in(key, 13)
    key_colour, key_end, key_mid = jax.random.split(key, 3)
    colours = jax.random.uniform(key_colour, (3, KNOTS), jnp.float32, 0.05, 1.0)
    ends = jax.random.uniform(key_end, (KNOTS,), jnp.float32, 0.5, 1.0)
    inner = jnp.exp(jax.random.uniform(key_mid, (KNOTS,), jnp.float32, jnp.log(0.001), jnp.log(0.01)))
    position = jnp.arange(KNOTS)
    at_end = (position == 0) | (position == KNOTS - 1)
    extinction = jnp.where(at_end, ends, inner)
    return jnp.concatenate([colours, extinction[None]], axis=0).astype(jnp.float32)


def place_ends(drawn, own_key, least, top_value):
    place = [jax.random.randint(jax.random.fold_in(own_key, axis), (), 0, length) for axis, length in enumerate(drawn.shape)]
    longest = drawn.shape.index(max(drawn.shape))
    beside = place[:longest] + [(place[longest] + 1) % drawn.shape[longest]] + place[longest + 1:]
    return drawn.at[tuple(place)].set(least).at[tuple(beside)].set(top_value)


def level_of(own_key, dims, pieces, smallest, largest):
    def one(axis_at, shards_of):
        draws = jax.random.uniform(jax.random.fold_in(jax.random.fold_in(own_key, 6), axis_at), (shards_of,), jnp.float32, smallest / len(pieces), largest / len(pieces))
        return jnp.repeat(jnp.exp(draws), dims[axis_at] // shards_of).reshape((-1,) + (1,) * (len(dims) - axis_at - 1))

    level = one(*pieces[0])
    for cut in pieces[1:]:
        level = level * one(*cut)
    return level


def centred(own_key, dims, spread, most, cuts=(), kind=jnp.bfloat16):
    gain = level_of(own_key, dims, cuts, -0.22, 0.18) if cuts else 1.0
    result = jax.random.normal(own_key, dims, jnp.float32) * spread * gain
    return jnp.minimum(jnp.maximum(result, -most), most).astype(kind)


def setup_inputs(seed: int = 0) -> dict:
    seeds = jax.random.split(jax.random.key(seed), 5)
    volume = centred(seeds[0], (NZ, NY, NX), 1.0, 6.0, ((0, 64), (1, 4)), jnp.float32)
    knot_bins = draw_knot_bins(jax.random.fold_in(seeds[4], 71), 0)
    colour_table = draw_colour_table(jax.random.fold_in(seeds[4], 71), 0)
    view_side = place_ends(jax.random.randint(seeds[3], (NX,), 0, 2), jax.random.fold_in(seeds[3], 1), 0, 1).astype(jnp.int32)
    return {"volume": volume, "knot_bins": knot_bins, "colour_table": colour_table, "view_side": view_side}


def axis_diff(values, axis):
    count = values.shape[axis]
    edge = jnp.zeros_like(lax.slice_in_dim(values, 0, 1, axis=axis))
    upper = jnp.concatenate([lax.slice_in_dim(values, 1, count, axis=axis), edge], axis=axis)
    lower_part = jnp.concatenate([edge, lax.slice_in_dim(values, 0, count - 1, axis=axis)], axis=axis)
    return (upper - lower_part) * 0.5

def sample_terms(centre, deriv_depth, deriv_rows, deriv_cols, knot_bins, colour_table, total_planes):
    sample = jnp.clip((centre + 3.0) / 6.0, 0.0, 1.0) * (BINS - 1)
    knot_pos = knot_bins.astype(jnp.float32)
    last = knot_bins.shape[0] - 2
    totals = [jnp.zeros_like(sample) for channel in range(4)]
    for knot in range(last + 1):
        lower_edge = knot_pos[knot]
        upper_edge = knot_pos[knot + 1]
        fraction = (sample - lower_edge) / (upper_edge - lower_edge)
        if knot == last:
            inside = (sample >= lower_edge) & (sample <= upper_edge)
        else:
            inside = (sample >= lower_edge) & (sample < upper_edge)
        for channel in range(4):
            start_value = colour_table[channel, knot]
            rising = colour_table[channel, knot + 1] - start_value
            totals[channel] = totals[channel] + jnp.where(inside, start_value + fraction * rising, 0.0)
    length = jnp.sqrt(deriv_depth * deriv_depth + deriv_rows * deriv_rows + deriv_cols * deriv_cols + 1.0)
    shading = 0.3 + 0.7 * jnp.abs(0.64 * deriv_depth + 0.6 * deriv_rows + 0.48 * deriv_cols) / length
    passed = jnp.exp(-totals[3] * (400.0 / total_planes))
    emitted = jnp.stack([(1.0 - passed) * totals[channel] * shading for channel in range(3)])
    return (passed, emitted)

def reference(volume, knot_bins, colour_table, view_side):
    toward = view_side == 1
    total_planes = volume.shape[0]

    def advance(carry, plane_index):
        colour, passing = carry
        centre = lax.dynamic_index_in_dim(volume, plane_index, 0, keepdims=False)
        under_index = jnp.maximum(plane_index - 1, 0).astype(jnp.int32)
        over_index = jnp.minimum(plane_index + 1, total_planes - 1).astype(jnp.int32)
        under_plane = lax.dynamic_index_in_dim(volume, under_index, 0, keepdims=False) * (plane_index > 0).astype(jnp.float32)
        over_plane = lax.dynamic_index_in_dim(volume, over_index, 0, keepdims=False) * (plane_index < total_planes - 1).astype(jnp.float32)
        deriv_depth = (over_plane - under_plane) * 0.5
        deriv_rows = axis_diff(centre, 0)
        deriv_cols = axis_diff(centre, 1)
        passed, emitted = sample_terms(centre, deriv_depth, deriv_rows, deriv_cols, knot_bins, colour_table, total_planes)
        colour = jnp.where(toward, colour + passing * emitted, emitted + passed * colour)
        passing = passing * passed
        return ((colour, passing), None)
    start = (jnp.zeros((3, NY, NX), jnp.float32), jnp.ones((NY, NX), jnp.float32))
    (colour, passing), unused = lax.scan(advance, start, jnp.arange(total_planes, dtype=jnp.int32))
    whole = jnp.concatenate([colour, (1.0 - passing)[None]], axis=0)
    whole = whole.reshape(4, N_TILE, N_SLAB, RB, NX)
    whole = jnp.transpose(whole, (0, 2, 1, 3, 4))
    return whole.reshape(4, N_SLAB, N_TILE * RB, NX)
```

```python
import jax
import jax.numpy as jnp
from jax import lax
from jax.experimental import pallas as pl
from jax.experimental.pallas import tpu as pltpu
from jax.sharding import PartitionSpec as P

BINS = 256
KNOTS = 8
LOG2_E = 1.4426950408889634
LANES = 128
ROWS = 8


def knot_tables(knot_bins, colour_table, total_planes):
    sublane = lax.broadcasted_iota(jnp.int32, (ROWS, LANES), 0)

    def spread(read):
        table = jnp.full((ROWS, LANES), read(0), jnp.float32)
        for knot in range(1, KNOTS):
            table = jnp.where(sublane == knot, read(knot), table)
        return table

    def position(knot):
        return knot_bins[knot].astype(jnp.float32)

    scale = 6.0 / (BINS - 1)
    knot_at = spread(position) * scale - 3.0
    knot_at = jnp.where(sublane == KNOTS - 1, 3.0, knot_at)
    width = pltpu.roll(knot_at, KNOTS - 1, 0) - knot_at
    starts, slopes = [], []
    for channel in range(4):
        start = spread(lambda knot: colour_table[channel, knot])
        rise = (pltpu.roll(start, KNOTS - 1, 0) - start) / width
        slope = jnp.where(sublane == KNOTS - 1, 0.0, rise)
        factor = -400.0 / total_planes * LOG2_E if channel == 3 else 1.0
        starts.append(start * factor)
        slopes.append(slope * factor)
    edges = [jnp.broadcast_to(knot_at[k : k + 1], (ROWS, LANES)) for k in range(KNOTS)]
    return knot_at, edges, starts, slopes


def look_up(value, tables):
    knot_at, edges, starts, slopes = tables
    index = jnp.zeros(value.shape, jnp.int32)
    for knot in range(1, KNOTS):
        index = jnp.where(value >= edges[knot], knot, index)

    def pick(table):
        return jnp.take_along_axis(table, index, axis=0, mode="promise_in_bounds")

    offset = value - pick(knot_at)
    return [pick(starts[c]) + offset * pick(slopes[c]) for c in range(4)]


def march_kernel(
    total_planes, core_ref, knot_ref, colour_ref, volume, above, below, row_prev, row_next, side_ref,
    send_ref, keep_ref, pad, stage, sems,
):
    planes, tile_rows, columns = volume.shape
    blocks = tile_rows // ROWS
    pieces = columns // LANES

    def fetch(block):
        rows = pl.ds(pl.multiple_of(block * ROWS, ROWS), ROWS)
        padded = pl.ds(pl.multiple_of(block * ROWS + ROWS, ROWS), ROWS)
        return pltpu.make_async_copy(volume.at[:, rows], pad.at[:, padded], sems.at[block])

    for block in range(blocks):
        fetch(block).start()
    for plane in range(planes):
        pad[plane, ROWS - 1 : ROWS, :] = row_prev[plane]
        pad[plane, ROWS + tile_rows : ROWS + tile_rows + 1, :] = row_next[plane]
    tables = knot_tables(knot_ref, colour_ref, total_planes)
    sublane = lax.broadcasted_iota(jnp.int32, (ROWS, LANES), 0)
    lane = lax.broadcasted_iota(jnp.int32, (ROWS, LANES), 1)
    zero = jnp.zeros((ROWS, LANES), jnp.float32)
    cols = [slice(p * LANES, (p + 1) * LANES) for p in range(pieces)]
    toward = [jnp.broadcast_to(side_ref[:, c], (ROWS, LANES)) == 1 for c in cols]
    fetch(0).wait()

    def row_block(block, carry):
        @pl.when(block < blocks - 1)
        def _():
            fetch(block + 1).wait()

        own = pl.ds(pl.multiple_of(block * ROWS, ROWS), ROWS)
        mid = pl.ds(pl.multiple_of(block * ROWS + ROWS, ROWS), ROWS)
        up = pl.ds(pl.multiple_of(block * ROWS, ROWS), ROWS)
        down = pl.ds(pl.multiple_of(block * ROWS + 2 * ROWS, ROWS), ROWS)
        colour = [[zero] * pieces for _ in range(3)]
        passing = [zero + 1.0] * pieces
        for plane in range(planes):
            here = [pad[plane, mid, c] for c in cols]
            to_left = [pltpu.roll(v, LANES - 1, 1) for v in here] + [zero]
            to_right = [zero] + [pltpu.roll(v, 1, 1) for v in here]
            for p, c in enumerate(cols):
                x = here[p]
                before = above[0, own, c] if plane == 0 else pad[plane - 1, mid, c]
                after = below[0, own, c] if plane == planes - 1 else pad[plane + 1, mid, c]
                depth = after - before
                row_up = pltpu.roll(jnp.where(sublane == ROWS - 1, pad[plane, up, c], x), 1, 0)
                row_down = pltpu.roll(jnp.where(sublane == 0, pad[plane, down, c], x), ROWS - 1, 0)
                rows = row_down - row_up
                col_up = jnp.where(lane == 0, to_right[p], to_right[p + 1])
                col_down = jnp.where(lane == LANES - 1, to_left[p + 1], to_left[p])
                across = col_down - col_up
                facing = jnp.abs(0.448 * depth + 0.42 * rows + 0.336 * across)
                square = depth * depth + rows * rows + (across * across + 4.0)
                shading = 0.3 + facing * lax.rsqrt(square)
                red, green, blue, exponent = look_up(jnp.minimum(jnp.maximum(x, -3.0), 3.0), tables)
                passed = jnp.exp2(exponent)
                fade = jnp.where(toward[p], 1.0, passed)
                weight = jnp.where(toward[p], passing[p], 1.0) * ((1.0 - passed) * shading)
                for channel, value in enumerate((red, green, blue)):
                    colour[channel][p] = colour[channel][p] * fade + weight * value
                passing[p] = passing[p] * passed
        for channel, parts in enumerate(colour + [passing]):
            for p in range(pieces):
                first = block * (ROWS * 4 * pieces) + channel * pieces + p
                stage[pl.ds(first, ROWS, stride=4 * pieces), :] = parts[p]
        return carry

    lax.fori_loop(0, blocks, row_block, 0)
    core = core_ref[0]
    unit = 4 * pieces
    for pair in range(tile_rows // 2):
        kept = pl.multiple_of((pair * 2 + core) * unit, unit)
        sent = pl.multiple_of((pair * 2 + 1 - core) * unit, unit)
        keep_ref[pair] = stage[pl.ds(kept, unit), :]
        send_ref[pair] = stage[pl.ds(sent, unit), :]


def pair_kernel(core_ref, mine, other, side_ref, out):
    count, unit, lanes = mine.shape
    quarter = unit // 4
    front = jnp.concatenate([side_ref[...]] * 4, axis=0) + core_ref[0] == 1
    for k in range(count):
        a, b = mine[k], other[k]
        first, second = jnp.where(front, a, b), jnp.where(front, b, a)
        passing = first[3 * quarter :]
        lead = jnp.concatenate([passing] * 4, axis=0)
        base = jnp.concatenate([first[: 3 * quarter], jnp.zeros_like(passing)], axis=0)
        out[k] = base + lead * second


def final_kernel(parts, side_ref, out):
    count, unit, lanes = parts.shape
    quarter = unit // 4
    toward = side_ref[...] == 1
    colour = jnp.zeros((3 * quarter, lanes), jnp.float32)
    passing = jnp.ones((quarter, lanes), jnp.float32)
    for k in range(count):
        value = parts[k]
        passed = value[3 * quarter :]
        fade = jnp.where(toward, 1.0, passed)
        weight = jnp.where(toward, passing, 1.0)
        colour = colour * jnp.concatenate([fade] * 3, 0) + value[: 3 * quarter] * jnp.concatenate([weight] * 3, 0)
        passing = passing * passed
    out[...] = jnp.concatenate([colour, 1.0 - passing], axis=0)


def per_device(volume, knot_bins, colour_table, view_side):
    planes, tile_rows, columns = volume.shape
    slabs, tiles = lax.axis_size("slab"), lax.axis_size("tile")
    core = (lax.axis_index("slab") & 1).astype(jnp.int32).reshape(1)
    pieces = columns // LANES
    unit = 4 * pieces
    half = tile_rows // 2

    def shift(block, axis, size, step):
        route = [(i, i + step) for i in range(size) if 0 <= i + step < size]
        return lax.ppermute(block, axis, route)

    row_prev = shift(volume[:, tile_rows - 1 :, :], "tile", tiles, 1)
    row_next = shift(volume[:, :1, :], "tile", tiles, -1)
    above = shift(volume[planes - 1 :], "slab", slabs, 1)
    below = shift(volume[:1], "slab", slabs, -1)

    vmem = pl.BlockSpec(memory_space=pltpu.VMEM)
    smem = pl.BlockSpec(memory_space=pltpu.SMEM)
    hbm = pl.BlockSpec(memory_space=pltpu.HBM)
    side_lanes = view_side.reshape(pieces, LANES)
    part = jax.ShapeDtypeStruct((half, unit, LANES), jnp.float32)

    def march(*refs):
        march_kernel(planes * slabs, *refs)

    send, keep = pl.pallas_call(
        march,
        out_shape=[part, part],
        in_specs=[smem, smem, smem, hbm, vmem, vmem, vmem, vmem, vmem],
        out_specs=[vmem, vmem],
        scratch_shapes=[
            pltpu.VMEM((planes, tile_rows + 2 * ROWS, columns), jnp.float32),
            pltpu.VMEM((tile_rows * unit, LANES), jnp.float32),
            pltpu.SemaphoreType.DMA((tile_rows // ROWS,)),
        ],
        compiler_params=pltpu.CompilerParams(vmem_limit_bytes=24 << 20),
        name="march",
    )(core, knot_bins, colour_table, volume, above, below, row_prev, row_next, view_side.reshape(1, columns))
    got = lax.ppermute(send, "slab", [(i, i ^ 1) for i in range(slabs)])
    merged = pl.pallas_call(
        pair_kernel,
        out_shape=part,
        in_specs=[smem, vmem, vmem, vmem],
        out_specs=vmem,
        name="pair",
    )(core, keep, got, side_lanes)
    groups = [[2 * q + c for q in range(slabs // 2)] for c in range(2)]
    parts = lax.all_to_all(merged, "slab", 0, 0, axis_index_groups=groups, tiled=True)
    image = pl.pallas_call(
        final_kernel,
        out_shape=jax.ShapeDtypeStruct((unit, LANES), jnp.float32),
        in_specs=[vmem, vmem],
        out_specs=vmem,
        name="final",
    )(parts, side_lanes)
    return image.reshape(4, 1, 1, columns)


def solution(mesh):
    return jax.shard_map(
        per_device,
        mesh=mesh,
        in_specs=(P("slab", "tile", None), P(), P(), P()),
        out_specs=P(None, "slab", "tile", None),
        check_vma=False,
    )
```

```python
import jax
import jax.numpy as jnp
from jax import lax
from jax.experimental import pallas as pl
from jax.experimental.pallas import tpu as pltpu
from jax.sharding import PartitionSpec as P

BINS = 256
KNOTS = 8
LOG2_E = 1.4426950408889634
LANES = 128
ROWS = 8
SMALL_VMEM = 4 << 20


def knot_tables(knot_bins, colour_table, total_planes):
    sublane = lax.broadcasted_iota(jnp.int32, (ROWS, LANES), 0)

    def spread(read):
        table = jnp.full((ROWS, LANES), read(0), jnp.float32)
        for knot in range(1, KNOTS):
            table = jnp.where(sublane == knot, read(knot), table)
        return table

    scale = 6.0 / (BINS - 1)
    knot_at = spread(lambda knot: knot_bins[knot].astype(jnp.float32)) * scale - 3.0
    knot_at = jnp.where(sublane == KNOTS - 1, 3.0, knot_at)
    width = pltpu.roll(knot_at, KNOTS - 1, 0) - knot_at
    starts, slopes = [], []
    for channel in range(4):
        start = spread(lambda knot: colour_table[channel, knot])
        rise = (pltpu.roll(start, KNOTS - 1, 0) - start) / width
        slope = jnp.where(sublane == KNOTS - 1, 0.0, rise)
        factor = -400.0 / total_planes * LOG2_E if channel == 3 else 1.0
        starts.append(start * factor)
        slopes.append(slope * factor)
    return [knot_at] + starts + slopes


def look_up(value, tables, edges):
    index = jnp.zeros(value.shape, jnp.int32)
    for knot in range(1, KNOTS):
        index = jnp.where(value >= edges[knot], knot, index)

    def pick(table):
        return jnp.take_along_axis(table, index, axis=0, mode="promise_in_bounds")

    offset = value - pick(tables[0])
    return [pick(tables[1 + c]) + offset * pick(tables[5 + c]) for c in range(4)]


def low_bits(axis, *bits):
    index = lax.axis_index(axis)
    return [(index >> bit) & 1 for bit in bits]


def load_kernel(
    total_planes, volume, knots_hbm, colours_hbm, side_hbm,
    pad, plane_near, plane_far, row_near, row_far, tables_ref, side_ref, knot_ref, colour_ref, sems, small_sems,
):
    planes, tile_rows, columns = volume.shape
    pieces = columns // LANES
    (core,), (tile,) = low_bits("slab", 0), low_bits("tile", 0)
    small = [
        pltpu.make_async_copy(knots_hbm, knot_ref, small_sems.at[0]),
        pltpu.make_async_copy(colours_hbm, colour_ref, small_sems.at[1]),
        pltpu.make_async_copy(side_hbm, side_ref, small_sems.at[2]),
    ]
    for copy in small:
        copy.start()
    fetches = []
    for plane in range(planes):
        for p in range(pieces):
            first = pad_row(pieces, tile_rows, plane + 1, p, 0)
            source = volume.at[plane, :, pl.ds(p * LANES, LANES)]
            sem = sems.at[plane * pieces + p]
            fetches.append(pltpu.make_async_copy(source, pad.at[pl.ds(first, tile_rows)], sem))
    for fetch in fetches:
        fetch.start()
    for copy in small:
        copy.wait()
    for k, table in enumerate(knot_tables(knot_ref, colour_ref, total_planes)):
        tables_ref[k] = table
    for fetch in fetches:
        fetch.wait()
    for k in range(planes * pieces // ROWS):
        first = pad_row(pieces, tile_rows, 1, k * ROWS, 0)
        stride = tile_rows + 2 * ROWS
        row_near[k] = pad[pl.ds(first + (tile_rows - 1) * (1 - tile), ROWS, stride=stride), :]
        row_far[k] = pad[pl.ds(first + (tile_rows - 1) * tile, ROWS, stride=stride), :]
    for p in range(pieces):
        near = pad_row(pieces, tile_rows, 1 + (planes - 1) * (1 - core), p, 0)
        far = pad_row(pieces, tile_rows, 1 + (planes - 1) * core, p, 0)
        plane_near[p] = pad[pl.ds(pl.multiple_of(near, ROWS), tile_rows), :]
        plane_far[p] = pad[pl.ds(pl.multiple_of(far, ROWS), tile_rows), :]


def pad_row(pieces, tile_rows, plane, piece, row):
    return (plane * pieces + piece) * (tile_rows + 2 * ROWS) + ROWS + row


def add_halo(pad, plane_near, plane_far, row_near, row_far):
    pieces, tile_rows, _ = plane_near.shape
    planes = row_near.shape[0] * ROWS // pieces
    (core,), (tile,) = low_bits("slab", 0), low_bits("tile", 0)
    for p in range(pieces):
        near = pad_row(pieces, tile_rows, (planes + 1) * (1 - core), p, 0)
        far = pad_row(pieces, tile_rows, (planes + 1) * core, p, 0)
        pad[pl.ds(pl.multiple_of(near, ROWS), tile_rows), :] = plane_near[p]
        pad[pl.ds(pl.multiple_of(far, ROWS), tile_rows), :] = plane_far[p]
    for k in range(row_near.shape[0]):
        first = pad_row(pieces, tile_rows, 1, k * ROWS, -1)
        stride = tile_rows + 2 * ROWS
        pad[pl.ds(first + (tile_rows + 1) * (1 - tile), ROWS, stride=stride), :] = row_near[k]
        pad[pl.ds(first + (tile_rows + 1) * tile, ROWS, stride=stride), :] = row_far[k]


def march(pad, tables_ref, side_ref, out, first_row, step, count):
    pieces = side_ref.shape[1] // LANES
    tile_rows = ROWS * ROWS
    planes = pad.shape[0] // (tile_rows + 2 * ROWS) // pieces - 2
    tables = [tables_ref[k] for k in range(tables_ref.shape[0])]
    edges = [jnp.broadcast_to(tables[0][k : k + 1], (ROWS, LANES)) for k in range(KNOTS)]
    lane = lax.broadcasted_iota(jnp.int32, (ROWS, LANES), 1)
    zero = jnp.zeros((ROWS, LANES), jnp.float32)
    cols = [slice(p * LANES, (p + 1) * LANES) for p in range(pieces)]
    toward = [jnp.broadcast_to(side_ref[:, c], (ROWS, LANES)) == 1 for c in cols]

    def group(j, carry):
        def read(plane, piece, shift=0):
            row = pad_row(pieces, tile_rows, plane, piece, first_row + step * j + shift)
            return pad[pl.ds(row, ROWS, stride=ROWS), :]

        colour = [[zero] * pieces for _ in range(3)]
        passing = [zero + 1.0] * pieces
        for plane in range(1, planes + 1):
            here = [read(plane, p) for p in range(pieces)]
            to_left = [pltpu.roll(v, LANES - 1, 1) for v in here] + [zero]
            to_right = [zero] + [pltpu.roll(v, 1, 1) for v in here]
            for p in range(pieces):
                x = here[p]
                depth = read(plane + 1, p) - read(plane - 1, p)
                rows = read(plane, p, 1) - read(plane, p, -1)
                col_up = jnp.where(lane == 0, to_right[p], to_right[p + 1])
                col_down = jnp.where(lane == LANES - 1, to_left[p + 1], to_left[p])
                across = col_down - col_up
                facing = jnp.abs(0.448 * depth + 0.42 * rows + 0.336 * across)
                square = depth * depth + rows * rows + (across * across + 4.0)
                shading = 0.3 + facing * lax.rsqrt(square)
                clipped = jnp.minimum(jnp.maximum(x, -3.0), 3.0)
                red, green, blue, exponent = look_up(clipped, tables, edges)
                passed = jnp.exp2(exponent)
                fade = jnp.where(toward[p], 1.0, passed)
                weight = jnp.where(toward[p], passing[p], 1.0) * ((1.0 - passed) * shading)
                for channel, value in enumerate((red, green, blue)):
                    colour[channel][p] = colour[channel][p] * fade + weight * value
                passing[p] = passing[p] * passed
        for channel, parts in enumerate(colour + [passing]):
            for p, c in enumerate(cols):
                out[j, channel, :, c] = parts[p]
        return carry

    lax.fori_loop(0, count, group, 0)


def merge(first_is_front, mine, other):
    lead = jnp.where(first_is_front, mine[3], other[3])
    merged = [
        jnp.where(first_is_front, mine[c], other[c]) + lead * jnp.where(first_is_front, other[c], mine[c])
        for c in range(3)
    ]
    return merged + [mine[3] * other[3]]


def both_halves(value):
    sublane = lax.broadcasted_iota(jnp.int32, value.shape, 0)
    return jnp.where(sublane < 4, pltpu.roll(value, 4, 0), value)


def final_kernel(parts, side_ref, out):
    toward = jnp.concatenate([side_ref[...]] * 2, axis=0) == 1
    lower = lax.broadcasted_iota(jnp.int32, (ROWS, LANES), 0) < 4
    top = bottom = jnp.zeros((ROWS, LANES), jnp.float32)
    passing = jnp.ones((ROWS, LANES), jnp.float32)
    for k in range(parts.shape[0]):
        passed = both_halves(parts[k, ROWS:])
        fade = jnp.where(toward, 1.0, passed)
        weight = jnp.where(toward, passing, 1.0)
        top = top * fade + parts[k, :ROWS] * weight
        bottom = bottom * fade + parts[k, ROWS:] * weight
        passing = passing * passed
    out[:ROWS] = top
    out[ROWS:] = jnp.where(lower, bottom, 1.0 - passing)


def per_device(volume, knot_bins, colour_table, view_side):
    planes, tile_rows, columns = volume.shape
    slabs, tiles = lax.axis_size("slab"), lax.axis_size("tile")
    pieces = columns // LANES
    unit = 4 * pieces
    groups = ROWS // 2

    vmem = pl.BlockSpec(memory_space=pltpu.VMEM)
    hbm = pl.BlockSpec(memory_space=pltpu.HBM)
    small = pltpu.CompilerParams(vmem_limit_bytes=SMALL_VMEM)

    def array(*shape):
        return jax.ShapeDtypeStruct(shape, jnp.float32)

    inputs = (volume, knot_bins, colour_table, view_side.reshape(1, columns))
    pad, *edges, tables, side = pl.pallas_call(
        lambda *refs: load_kernel(planes * slabs, *refs),
        out_shape=[
            pltpu.VMEM(((planes + 2) * pieces * (tile_rows + 2 * ROWS), LANES), jnp.float32),
            *[pltpu.VMEM((pieces, tile_rows, LANES), jnp.float32)] * 2,
            *[pltpu.VMEM((planes * pieces // ROWS, ROWS, LANES), jnp.float32)] * 2,
            pltpu.VMEM((9, ROWS, LANES), jnp.float32),
            pltpu.VMEM((1, columns), jnp.int32),
        ],
        in_specs=[hbm] * 4,
        out_specs=[vmem] * 7,
        scratch_shapes=[
            pltpu.SMEM((KNOTS,), jnp.int32),
            pltpu.SMEM((4, KNOTS), jnp.float32),
            pltpu.SemaphoreType.DMA((planes * pieces,)),
            pltpu.SemaphoreType.DMA((3,)),
        ],
        compiler_params=pltpu.CompilerParams(vmem_limit_bytes=SMALL_VMEM),
        name="load",
    )(*[pltpu.with_memory_space_constraint(x, pltpu.HBM) for x in inputs])

    def swap(block, axis, size, low):
        route = [(i, i + 1) for i in range(low, size - 1, 2)]
        return lax.ppermute(block, axis, route + [(j, i) for i, j in route])

    halo = [
        swap(edges[0], "slab", slabs, 0),
        swap(edges[1], "slab", slabs, 1),
        swap(edges[2], "tile", tiles, 0),
        swap(edges[3], "tile", tiles, 1),
    ]

    def cost(share):
        count = planes * tile_rows * columns // share
        return pl.CostEstimate(flops=100 * count, bytes_accessed=16 * count, transcendentals=2 * count)

    def march_sent(pad_in, near, far, row_near, row_far, tables, side, pad, out):
        add_halo(pad, near, far, row_near, row_far)
        (core,) = low_bits("slab", 0)
        march(pad, tables, side, out, 1 - core, 2, groups)

    def march_kept(pad, tables, side, out):
        (core,) = low_bits("slab", 0)
        march(pad, tables, side, out, core, 2, groups)

    half = array(groups, 4, ROWS, columns)
    pad, sent = pl.pallas_call(
        march_sent,
        out_shape=[array(*pad.shape), half],
        in_specs=[vmem] * 7,
        out_specs=[vmem] * 2,
        input_output_aliases={0: 0},
        compiler_params=small,
        cost_estimate=cost(2),
        name="march_sent",
    )(pad, *halo, tables, side)
    got = lax.ppermute(sent, "slab", [(i, i ^ 1) for i in range(slabs)])
    kept = pl.pallas_call(
        march_kept,
        out_shape=half,
        in_specs=[vmem] * 3,
        out_specs=vmem,
        compiler_params=small,
        cost_estimate=cost(2),
        name="march_kept",
    )(pad, tables, side)

    def pair(mine, other, side_ref, out):
        (core,) = low_bits("slab", 0)
        for p in range(pieces):
            c = slice(p * LANES, (p + 1) * LANES)
            front = jnp.broadcast_to(side_ref[:, c], (ROWS, LANES)) + core == 1
            for x in range(groups):
                whole = merge(front, [mine[x, k, :, c] for k in range(4)], [other[x, k, :, c] for k in range(4)])
                for k, value in enumerate(whole):
                    out[pl.ds(x * unit + k * pieces + p, ROWS, stride=groups * unit), :] = value

    merged = pl.pallas_call(
        pair,
        out_shape=array(ROWS * groups * unit, LANES),
        in_specs=[vmem] * 3,
        out_specs=vmem,
        compiler_params=small,
        name="pair",
    )(kept, got, side)
    members = [[2 * q + c for q in range(slabs // 2)] for c in range(2)]
    parts = lax.all_to_all(
        merged.reshape(slabs // 2, unit, LANES), "slab", 0, 0, axis_index_groups=members, tiled=True
    )
    image = pl.pallas_call(
        final_kernel,
        out_shape=array(unit, LANES),
        in_specs=[vmem] * 2,
        out_specs=vmem,
        compiler_params=small,
        name="final",
    )(parts, side.reshape(pieces, LANES))
    return image.reshape(4, 1, 1, columns)


def solution(mesh):
    return jax.shard_map(
        per_device,
        mesh=mesh,
        in_specs=(P("slab", "tile", None), P(), P(), P()),
        out_specs=P(None, "slab", "tile", None),
        check_vma=False,
    )
```

```python
import jax
import jax.numpy as jnp
from jax import lax
from jax.experimental import pallas as pl
from jax.experimental.pallas import tpu as pltpu
from jax.sharding import PartitionSpec as P

BINS = 256
KNOTS = 8
LOG2_E = 1.4426950408889634
LANES = 128
ROWS = 8
SMALL_VMEM = 4 << 20
LOAD_PARTS = 1
INNER_UNROLL = 2


def knot_tables(knot_bins, colour_table, total_planes):
    sublane = lax.broadcasted_iota(jnp.int32, (ROWS, LANES), 0)

    def spread(read):
        table = jnp.full((ROWS, LANES), read(0), jnp.float32)
        for knot in range(1, KNOTS):
            table = jnp.where(sublane == knot, read(knot), table)
        return table

    scale = 6.0 / (BINS - 1)
    knot_at = spread(lambda knot: knot_bins[knot].astype(jnp.float32)) * scale - 3.0
    knot_at = jnp.where(sublane == KNOTS - 1, 3.0, knot_at)
    width = pltpu.roll(knot_at, KNOTS - 1, 0) - knot_at
    starts, slopes = [], []
    for channel in range(4):
        start = spread(lambda knot: colour_table[channel, knot])
        rise = (pltpu.roll(start, KNOTS - 1, 0) - start) / width
        slope = jnp.where(sublane == KNOTS - 1, 0.0, rise)
        factor = -400.0 / total_planes * LOG2_E if channel == 3 else 1.0
        starts.append(start * factor)
        slopes.append(slope * factor)
    return [knot_at] + starts + slopes


def look_up(value, tables, edges):
    index = jnp.zeros(value.shape, jnp.int32)
    for knot in range(1, KNOTS - 1):
        index = jnp.where(value >= edges[knot], knot, index)

    def pick(table):
        return jnp.take_along_axis(table, index, axis=0, mode="promise_in_bounds")

    offset = value - pick(tables[0])
    return [pick(tables[1 + c]) + offset * pick(tables[5 + c]) for c in range(4)]


def low_bits(axis, *bits):
    index = lax.axis_index(axis)
    return [(index >> bit) & 1 for bit in bits]


def load_kernel(
    total_planes, volume, knots_hbm, colours_hbm, side_hbm,
    pad, plane_near, plane_far, row_near, row_far, tables_ref, side_ref, knot_ref, colour_ref, sems, small_sems,
):
    planes, tile_rows, columns = volume.shape
    pieces = columns // LANES
    (core,), (tile,) = low_bits("slab", 0), low_bits("tile", 0)
    small = [
        pltpu.make_async_copy(knots_hbm, knot_ref, small_sems.at[0]),
        pltpu.make_async_copy(colours_hbm, colour_ref, small_sems.at[1]),
        pltpu.make_async_copy(side_hbm, side_ref, small_sems.at[2]),
    ]
    fetches = []
    share = planes // LOAD_PARTS
    for k in range(LOAD_PARTS):
        for p in range(pieces):
            source = volume.at[pl.ds(k * share, share), :, pl.ds(p * LANES, LANES)]
            target = pad.at[pl.ds(k * share + 1, share), pl.ds(pad_row(tile_rows, p, 0), tile_rows)]
            fetches.append(pltpu.make_async_copy(source, target, sems.at[k * pieces + p]))
    for copy in small + fetches:
        copy.start()
    for copy in small:
        copy.wait()
    for k, table in enumerate(knot_tables(knot_ref, colour_ref, total_planes)):
        tables_ref[k] = table
    for fetch in fetches:
        fetch.wait()
    stride = tile_rows + 2 * ROWS
    near, far = [pad_row(tile_rows, 0, 0) + (tile_rows - 1) * at for at in (1 - tile, tile)]
    for plane in range(planes):
        row_near[plane] = pad[plane + 1, pl.ds(near, pieces, stride=stride), :]
        row_far[plane] = pad[plane + 1, pl.ds(far, pieces, stride=stride), :]
    for p in range(pieces):
        rows = slice(pad_row(tile_rows, p, 0), pad_row(tile_rows, p, tile_rows))
        lanes = slice(p * LANES, (p + 1) * LANES)
        plane_near[0, :, lanes] = pad[1 + (planes - 1) * (1 - core), rows, :]
        plane_far[0, :, lanes] = pad[1 + (planes - 1) * core, rows, :]


def pad_row(tile_rows, piece, row):
    return piece * (tile_rows + 2 * ROWS) + ROWS + row


def add_halo(pad, plane_near, plane_far, row_near, row_far):
    _, tile_rows, columns = plane_near.shape
    planes, pieces, _ = row_near.shape
    (core,), (tile,) = low_bits("slab", 0), low_bits("tile", 0)
    for p in range(pieces):
        lanes = slice(p * LANES, (p + 1) * LANES)
        rows = slice(pad_row(tile_rows, p, 0), pad_row(tile_rows, p, tile_rows))
        pad[(planes + 1) * (1 - core), rows, :] = plane_near[0, :, lanes]
        pad[(planes + 1) * core, rows, :] = plane_far[0, :, lanes]
    first, stride = pad_row(tile_rows, 0, -1), tile_rows + 2 * ROWS
    for plane in range(planes):
        pad[plane + 1, pl.ds(first + (tile_rows + 1) * (1 - tile), pieces, stride=stride), :] = row_near[plane]
        pad[plane + 1, pl.ds(first + (tile_rows + 1) * tile, pieces, stride=stride), :] = row_far[plane]


class Marcher:
    def __init__(self, pad, tables_ref, side_ref):
        self.pad = pad
        self.pieces = side_ref.shape[1] // LANES
        self.planes = pad.shape[0] - 2
        self.tables = [tables_ref[k] for k in range(tables_ref.shape[0])]
        at = self.tables[0]
        self.edges = [jnp.broadcast_to(at[k : k + 1], (ROWS, LANES)) for k in range(KNOTS)]
        self.lane = lax.broadcasted_iota(jnp.int32, (ROWS, LANES), 1)
        self.lanes = [slice(p * LANES, (p + 1) * LANES) for p in range(self.pieces)]
        sides = [jnp.broadcast_to(side_ref[:, c], (ROWS, LANES)) for c in self.lanes]
        self.toward = [side == 1 for side in sides]
        self.away = [side != 1 for side in sides]

    def read(self, group, plane, piece, shift=0):
        row = pad_row(ROWS * ROWS, piece, group + shift)
        return self.pad[plane + 1, pl.ds(row, ROWS, stride=ROWS), :]

    def start(self):
        zero = jnp.zeros((ROWS, LANES), jnp.float32)
        return [[zero] * self.pieces for _ in range(3)] + [[zero + 1.0] * self.pieces]

    def load(self, ref):
        return [[ref[k, :, c] for c in self.lanes] for k in range(4)]

    def store(self, ref, state):
        for k in range(4):
            for p, c in enumerate(self.lanes):
                ref[k, :, c] = state[k][p]

    def steps(self, state, group, planes, onward):
        held = {}
        for plane in planes:
            held = {
                q: held[q] if q in held else [self.read(group, q, p) for p in range(self.pieces)]
                for q in range(plane - 1, plane + 2)
            }
            state = self.step(state, group, plane, onward, *[held[plane + d] for d in (-1, 0, 1)])
        return state

    def step(self, state, group, plane, onward, before, here, after):
        lane, zero = self.lane, jnp.zeros((ROWS, LANES), jnp.float32)
        to_left = [pltpu.roll(v, LANES - 1, 1) for v in here] + [zero]
        to_right = [zero] + [pltpu.roll(v, 1, 1) for v in here]
        new = [[], [], [], []]
        for p, x in enumerate(here):
            depth = after[p] - before[p]
            rows = self.read(group, plane, p, 1) - self.read(group, plane, p, -1)
            col_up = jnp.where(lane == 0, to_right[p], to_right[p + 1])
            col_down = jnp.where(lane == LANES - 1, to_left[p + 1], to_left[p])
            across = col_down - col_up
            facing = jnp.abs(0.448 * depth + 0.42 * rows + 0.336 * across)
            square = depth * depth + rows * rows + (across * across + 4.0)
            shading = 0.3 + facing * lax.rsqrt(square)
            clipped = jnp.minimum(jnp.maximum(x, -3.0), 3.0)
            red, green, blue, exponent = look_up(clipped, self.tables, self.edges)
            passed = jnp.exp2(exponent)
            fade = jnp.where(onward[p], 1.0, passed)
            weight = jnp.where(onward[p], state[3][p], 1.0) * ((1.0 - passed) * shading)
            for channel, value in enumerate((red, green, blue)):
                new[channel].append(state[channel][p] * fade + weight * value)
            new[3].append(state[3][p] * passed)
        return new


def inner_kernel(pad, tables_ref, side_ref, states):
    marcher = Marcher(pad, tables_ref, side_ref)

    def group(j, carry):
        state = marcher.steps(marcher.start(), 1 + j, range(1, marcher.planes - 1), marcher.toward)
        marcher.store(states.at[1 + j], state)
        return carry

    lax.fori_loop(0, ROWS - 2, group, 0, unroll=INNER_UNROLL)


def finish(pad, states, tables_ref, side_ref, out, parity):
    marcher = Marcher(pad, tables_ref, side_ref)
    outermost = parity * (ROWS - 1)
    state = marcher.start()
    state = marcher.steps(state, outermost, range(marcher.planes), marcher.toward)
    marcher.store(out.at[parity * (ROWS // 2 - 1)], state)

    def group(j, carry):
        g = 2 - parity + 2 * j
        state = marcher.load(states.at[g])
        state = marcher.steps(state, g, [marcher.planes - 1], marcher.toward)
        state = marcher.steps(state, g, [0], marcher.away)
        marcher.store(out.at[1 - parity + j], state)
        return carry

    lax.fori_loop(0, ROWS // 2 - 1, group, 0, unroll=True)


def merge(first_is_front, mine, other):
    lead = jnp.where(first_is_front, mine[3], other[3])
    merged = [
        jnp.where(first_is_front, mine[c], other[c]) + lead * jnp.where(first_is_front, other[c], mine[c])
        for c in range(3)
    ]
    return merged + [mine[3] * other[3]]


def both_halves(value):
    sublane = lax.broadcasted_iota(jnp.int32, value.shape, 0)
    return jnp.where(sublane < 4, pltpu.roll(value, 4, 0), value)


def final_kernel(parts, side_ref, out):
    toward = jnp.concatenate([side_ref[...]] * 2, axis=0) == 1
    lower = lax.broadcasted_iota(jnp.int32, (ROWS, LANES), 0) < 4
    top = bottom = jnp.zeros((ROWS, LANES), jnp.float32)
    passing = jnp.ones((ROWS, LANES), jnp.float32)
    for k in range(parts.shape[0]):
        passed = both_halves(parts[k, ROWS:])
        fade = jnp.where(toward, 1.0, passed)
        weight = jnp.where(toward, passing, 1.0)
        top = top * fade + parts[k, :ROWS] * weight
        bottom = bottom * fade + parts[k, ROWS:] * weight
        passing = passing * passed
    out[:ROWS] = top
    out[ROWS:] = jnp.where(lower, bottom, 1.0 - passing)


def per_device(volume, knot_bins, colour_table, view_side):
    planes, tile_rows, columns = volume.shape
    slabs, tiles = lax.axis_size("slab"), lax.axis_size("tile")
    pieces = columns // LANES
    unit = 4 * pieces
    groups = ROWS // 2

    vmem = pl.BlockSpec(memory_space=pltpu.VMEM)
    hbm = pl.BlockSpec(memory_space=pltpu.HBM)
    small = pltpu.CompilerParams(vmem_limit_bytes=SMALL_VMEM)

    def array(*shape):
        return jax.ShapeDtypeStruct(shape, jnp.float32)

    inputs = (volume, knot_bins, colour_table, view_side.reshape(1, columns))
    inputs = [pltpu.with_memory_space_constraint(x, pltpu.HBM) for x in inputs]
    plane = pltpu.VMEM((1, tile_rows, columns), jnp.float32)
    row = pltpu.VMEM((planes, pieces, LANES), jnp.float32)
    pad, *edges, tables, side = pl.pallas_call(
        lambda *refs: load_kernel(planes * slabs, *refs),
        out_shape=[
            pltpu.VMEM((planes + 2, pieces * (tile_rows + 2 * ROWS), LANES), jnp.float32),
            plane, plane, row, row,
            pltpu.VMEM((9, ROWS, LANES), jnp.float32),
            pltpu.VMEM((1, columns), jnp.int32),
        ],
        in_specs=[hbm] * 4,
        out_specs=[vmem] * 7,
        scratch_shapes=[
            pltpu.SMEM((KNOTS,), jnp.int32),
            pltpu.SMEM((4, KNOTS), jnp.float32),
            pltpu.SemaphoreType.DMA((LOAD_PARTS * pieces,)),
            pltpu.SemaphoreType.DMA((3,)),
        ],
        compiler_params=small,
        name="load",
    )(*inputs)

    def swap(block, axis, size, low):
        route = [(i, i + 1) for i in range(low, size - 1, 2)]
        return lax.ppermute(block, axis, route + [(j, i) for i, j in route])

    halo = [
        swap(edges[0], "slab", slabs, 0),
        swap(edges[1], "slab", slabs, 1),
        swap(edges[2], "tile", tiles, 0),
        swap(edges[3], "tile", tiles, 1),
    ]

    def cost(steps):
        count = steps * ROWS * columns
        return pl.CostEstimate(flops=100 * count, bytes_accessed=16 * count, transcendentals=2 * count)

    inner = (ROWS - 2) * (planes - 2)
    outer = (ROWS * planes - inner) // 2
    states = pl.pallas_call(
        inner_kernel,
        out_shape=array(ROWS, 4, ROWS, columns),
        in_specs=[vmem] * 3,
        out_specs=vmem,
        compiler_params=small,
        cost_estimate=cost(inner),
        name="inner",
    )(pad, tables, side)

    def finish_sent(pad_in, near, far, row_near, row_far, states, tables, side, pad, out):
        add_halo(pad, near, far, row_near, row_far)
        (core,) = low_bits("slab", 0)
        finish(pad, states, tables, side, out, 1 - core)

    def finish_kept(pad, states, tables, side, out):
        (core,) = low_bits("slab", 0)
        finish(pad, states, tables, side, out, core)

    half = array(groups, 4, ROWS, columns)
    pad, sent = pl.pallas_call(
        finish_sent,
        out_shape=[array(*pad.shape), half],
        in_specs=[vmem] * 8,
        out_specs=[vmem] * 2,
        input_output_aliases={0: 0},
        compiler_params=small,
        cost_estimate=cost(outer),
        name="finish_sent",
    )(pad, *halo, states, tables, side)
    got = lax.ppermute(sent, "slab", [(i, i ^ 1) for i in range(slabs)])
    kept = pl.pallas_call(
        finish_kept,
        out_shape=half,
        in_specs=[vmem] * 4,
        out_specs=vmem,
        compiler_params=small,
        cost_estimate=cost(outer),
        name="finish_kept",
    )(pad, states, tables, side)

    def pair(mine, other, side_ref, out):
        (core,) = low_bits("slab", 0)
        for p in range(pieces):
            c = slice(p * LANES, (p + 1) * LANES)
            front = jnp.broadcast_to(side_ref[:, c], (ROWS, LANES)) + core == 1
            for x in range(groups):
                whole = merge(front, [mine[x, k, :, c] for k in range(4)], [other[x, k, :, c] for k in range(4)])
                for k, value in enumerate(whole):
                    out[pl.ds(x * unit + k * pieces + p, ROWS, stride=groups * unit), :] = value

    merged = pl.pallas_call(
        pair,
        out_shape=array(ROWS * groups * unit, LANES),
        in_specs=[vmem] * 3,
        out_specs=vmem,
        compiler_params=small,
        name="pair",
    )(kept, got, side)
    members = [[2 * q + c for q in range(slabs // 2)] for c in range(2)]
    parts = lax.all_to_all(
        merged.reshape(slabs // 2, unit, LANES), "slab", 0, 0, axis_index_groups=members, tiled=True
    )
    image = pl.pallas_call(
        final_kernel,
        out_shape=array(unit, LANES),
        in_specs=[vmem] * 2,
        out_specs=vmem,
        compiler_params=small,
        name="final",
    )(parts, side.reshape(pieces, LANES))
    return image.reshape(4, 1, 1, columns)


def solution(mesh):
    return jax.shard_map(
        per_device,
        mesh=mesh,
        in_specs=(P("slab", "tile", None), P(), P(), P()),
        out_specs=P(None, "slab", "tile", None),
        check_vma=False,
    )
```

```python
import jax
import jax.numpy as jnp
from jax import lax
from jax.experimental import pallas as pl
from jax.experimental.pallas import tpu as pltpu
from jax.sharding import PartitionSpec as P

BINS = 256
KNOTS = 8
LOG2_E = 1.4426950408889634
LANES = 128
ROWS = 8
SMALL_VMEM = 4 << 20
FACING = 0.7 * 0.64
LOAD_PARTS = 1
INNER_UNROLL = 5


def knot_tables(knot_bins, colour_table, total_planes):
    sublane = lax.broadcasted_iota(jnp.int32, (ROWS, LANES), 0)

    def spread(read):
        table = jnp.full((ROWS, LANES), read(0), jnp.float32)
        for knot in range(1, KNOTS):
            table = jnp.where(sublane == knot, read(knot), table)
        return table

    scale = 6.0 / (BINS - 1)
    knot_at = spread(lambda knot: knot_bins[knot].astype(jnp.float32)) * scale - 3.0
    knot_at = jnp.where(sublane == KNOTS - 1, 3.0, knot_at)
    width = pltpu.roll(knot_at, KNOTS - 1, 0) - knot_at
    starts, slopes = [], []
    for channel in range(4):
        start = spread(lambda knot: colour_table[channel, knot])
        rise = (pltpu.roll(start, KNOTS - 1, 0) - start) / width
        slope = jnp.where(sublane == KNOTS - 1, 0.0, rise)
        factor = -400.0 / total_planes * LOG2_E if channel == 3 else FACING
        starts.append(start * factor)
        slopes.append(slope * factor)
    return [knot_at] + starts + slopes


def look_up(value, tables, edges):
    index = jnp.zeros(value.shape, jnp.int32)
    for knot in range(1, KNOTS - 1):
        index = jnp.where(value >= edges[knot], knot, index)

    def pick(table):
        return jnp.take_along_axis(table, index, axis=0, mode="promise_in_bounds")

    offset = value - pick(tables[0])
    return [pick(tables[1 + c]) + offset * pick(tables[5 + c]) for c in range(4)]


def low_bits(axis, *bits):
    index = lax.axis_index(axis)
    return [(index >> bit) & 1 for bit in bits]


def load_kernel(
    total_planes, volume, knots_hbm, colours_hbm, side_hbm,
    pad, plane_near, plane_far, row_near, row_far, tables_ref, side_ref, knot_ref, colour_ref, sems, small_sems,
):
    planes, tile_rows, columns = volume.shape
    pieces = columns // LANES
    (core,), (tile,) = low_bits("slab", 0), low_bits("tile", 0)
    small = [
        pltpu.make_async_copy(knots_hbm, knot_ref, small_sems.at[0]),
        pltpu.make_async_copy(colours_hbm, colour_ref, small_sems.at[1]),
        pltpu.make_async_copy(side_hbm, side_ref, small_sems.at[2]),
    ]
    fetches = []
    share = planes // LOAD_PARTS
    for k in range(LOAD_PARTS):
        for p in range(pieces):
            source = volume.at[pl.ds(k * share, share), :, pl.ds(p * LANES, LANES)]
            target = pad.at[pl.ds(k * share + 1, share), pl.ds(pad_row(tile_rows, p, 0), tile_rows)]
            fetches.append(pltpu.make_async_copy(source, target, sems.at[k * pieces + p]))
    for copy in small + fetches:
        copy.start()
    for copy in small:
        copy.wait()
    for k, table in enumerate(knot_tables(knot_ref, colour_ref, total_planes)):
        tables_ref[k] = table
    for fetch in fetches:
        fetch.wait()
    stride = tile_rows + 2 * ROWS
    near, far = [pad_row(tile_rows, 0, 0) + (tile_rows - 1) * at for at in (1 - tile, tile)]
    for plane in range(planes):
        row_near[plane] = pad[plane + 1, pl.ds(near, pieces, stride=stride), :]
        row_far[plane] = pad[plane + 1, pl.ds(far, pieces, stride=stride), :]
    for p in range(pieces):
        rows = slice(pad_row(tile_rows, p, 0), pad_row(tile_rows, p, tile_rows))
        lanes = slice(p * LANES, (p + 1) * LANES)
        plane_near[0, :, lanes] = pad[1 + (planes - 1) * (1 - core), rows, :]
        plane_far[0, :, lanes] = pad[1 + (planes - 1) * core, rows, :]


def pad_row(tile_rows, piece, row):
    return piece * (tile_rows + 2 * ROWS) + ROWS + row


def add_halo(pad, plane_near, plane_far, row_near, row_far):
    _, tile_rows, columns = plane_near.shape
    planes, pieces, _ = row_near.shape
    (core,), (tile,) = low_bits("slab", 0), low_bits("tile", 0)
    for p in range(pieces):
        lanes = slice(p * LANES, (p + 1) * LANES)
        rows = slice(pad_row(tile_rows, p, 0), pad_row(tile_rows, p, tile_rows))
        pad[(planes + 1) * (1 - core), rows, :] = plane_near[0, :, lanes]
        pad[(planes + 1) * core, rows, :] = plane_far[0, :, lanes]
    first, stride = pad_row(tile_rows, 0, -1), tile_rows + 2 * ROWS
    for plane in range(planes):
        pad[plane + 1, pl.ds(first + (tile_rows + 1) * (1 - tile), pieces, stride=stride), :] = row_near[plane]
        pad[plane + 1, pl.ds(first + (tile_rows + 1) * tile, pieces, stride=stride), :] = row_far[plane]


class Marcher:
    def __init__(self, pad, tables_ref, side_ref, stash):
        self.pad, self.stash = pad, stash
        self.pieces = side_ref.shape[1] // LANES
        self.planes = pad.shape[0] - 2
        self.tables = [tables_ref[k] for k in range(tables_ref.shape[0])]
        at = self.tables[0]
        self.edges = [jnp.broadcast_to(at[k : k + 1], (ROWS, LANES)) for k in range(KNOTS)]
        self.lane = lax.broadcasted_iota(jnp.int32, (ROWS, LANES), 1)
        self.lanes = [slice(p * LANES, (p + 1) * LANES) for p in range(self.pieces)]
        self.toward = [jnp.broadcast_to(side_ref[:, c], (ROWS, LANES)) == 1 for c in self.lanes]

    def read(self, group, plane, piece, shift=0):
        row = pad_row(ROWS * ROWS, piece, group + shift)
        return self.pad[plane + 1, pl.ds(row, ROWS, stride=ROWS), :]

    def start(self):
        zero = jnp.zeros((ROWS, LANES), jnp.float32)
        return [[zero] * self.pieces for _ in range(3)] + [[zero + 1.0] * self.pieces]

    def load(self, ref):
        return [[ref[k, :, c] for c in self.lanes] for k in range(4)]

    def store(self, ref, state):
        for k in range(4):
            for p, c in enumerate(self.lanes):
                ref[k, :, c] = state[k][p]

    def shade(self, group, plane, held):
        lane, zero = self.lane, jnp.zeros((ROWS, LANES), jnp.float32)
        for q in range(plane - 1, plane + 2):
            if q not in held:
                held[q] = [self.read(group, q, p) for p in range(self.pieces)]
        before, here, after = [held[plane + d] for d in (-1, 0, 1)]
        to_left = [pltpu.roll(v, LANES - 1, 1) for v in here] + [zero]
        to_right = [zero] + [pltpu.roll(v, 1, 1) for v in here]
        strengths = []
        for p in range(self.pieces):
            depth = after[p] - before[p]
            rows = self.read(group, plane, p, 1) - self.read(group, plane, p, -1)
            col_up = jnp.where(lane == 0, to_right[p], to_right[p + 1])
            col_down = jnp.where(lane == LANES - 1, to_left[p + 1], to_left[p])
            across = col_down - col_up
            facing = jnp.abs(depth + (0.6 / 0.64) * rows + (0.48 / 0.64) * across)
            square = depth * depth + rows * rows + (across * across + 4.0)
            strengths.append(0.3 / FACING + facing * lax.rsqrt(square))
        return here, strengths

    def pair(self, group, plane, held):
        (low, low_strength), (high, high_strength) = [
            self.shade(group, q, held) for q in (plane, self.planes - 1 - plane)
        ]
        near, far = [], []
        for p, toward in enumerate(self.toward):
            near.append((jnp.where(toward, low[p], high[p]), jnp.where(toward, low_strength[p], high_strength[p])))
            far.append((jnp.where(toward, high[p], low[p]), jnp.where(toward, high_strength[p], low_strength[p])))
        return near, far

    def behind(self, state, plane):
        new = [[], [], [], []]
        for p, (x, strength) in enumerate(plane):
            clipped = jnp.minimum(jnp.maximum(x, -3.0), 3.0)
            red, green, blue, exponent = look_up(clipped, self.tables, self.edges)
            left = state[3][p] * jnp.exp2(exponent)
            weight = (state[3][p] - left) * strength
            for channel, value in enumerate((red, green, blue)):
                new[channel].append(state[channel][p] + weight * value)
            new[3].append(left)
        return new

    def run(self, group, first):
        state, held = self.start(), {}
        for plane in range(first, self.planes // 2):
            near, far = self.pair(group, plane, held)
            state = self.behind(state, near)
            for p in range(self.pieces):
                for k in range(2):
                    self.stash[(plane * self.pieces + p) * 2 + k] = far[p][k]
        for plane in reversed(range(first, self.planes // 2)):
            at = [(plane * self.pieces + p) * 2 for p in range(self.pieces)]
            state = self.behind(state, [(self.stash[k], self.stash[k + 1]) for k in at])
        return state

    def ends(self, state, group):
        near, far = self.pair(group, 0, {})
        front = self.behind(self.start(), near)
        state = [
            [front[k][p] + front[3][p] * state[k][p] if k < 3 else front[3][p] * state[3][p] for p in range(self.pieces)]
            for k in range(4)
        ]
        return self.behind(state, far)


def late_group(parity):
    return ROWS - 2 - parity


def inner_kernel(pad, tables_ref, side_ref, states, stash):
    marcher = Marcher(pad, tables_ref, side_ref, stash)
    (core,) = low_bits("slab", 0)

    def group(j, carry):
        g = 1 + j + (1 + j >= late_group(core)).astype(jnp.int32)
        marcher.store(states.at[g], marcher.run(g, 1))
        return carry

    lax.fori_loop(0, ROWS - 3, group, 0, unroll=INNER_UNROLL)


def finish(pad, states, tables_ref, side_ref, out, stash, parity, left):
    marcher = Marcher(pad, tables_ref, side_ref, stash)

    def whole(t, carry):
        g = jnp.where(t == 0, parity * (ROWS - 1), late_group(parity))
        marcher.store(out.at[g >> 1], marcher.run(g, 0))
        return carry

    def group(j, carry):
        g = 2 - parity + 2 * j
        marcher.store(out.at[g >> 1], marcher.ends(marcher.load(states.at[g]), g))
        return carry

    lax.fori_loop(0, left, whole, 0, unroll=True)
    lax.fori_loop(0, ROWS // 2 - left, group, 0, unroll=True)


def merge(first_is_front, mine, other):
    lead = jnp.where(first_is_front, mine[3], other[3])
    merged = [
        jnp.where(first_is_front, mine[c], other[c]) + lead * jnp.where(first_is_front, other[c], mine[c])
        for c in range(3)
    ]
    return merged + [mine[3] * other[3]]


def both_halves(value):
    sublane = lax.broadcasted_iota(jnp.int32, value.shape, 0)
    return jnp.where(sublane < 4, pltpu.roll(value, 4, 0), value)


def final_kernel(parts, side_ref, out):
    toward = jnp.concatenate([side_ref[...]] * 2, axis=0) == 1
    lower = lax.broadcasted_iota(jnp.int32, (ROWS, LANES), 0) < 4
    whole = [(parts[k, :ROWS], parts[k, ROWS:], both_halves(parts[k, ROWS:])) for k in range(parts.shape[0])]
    while len(whole) > 1:
        joined = []
        for (top, bottom, passing), (top_2, bottom_2, passing_2) in zip(whole[::2], whole[1::2]):
            lead = jnp.where(toward, passing, passing_2)
            joined.append((
                jnp.where(toward, top, top_2) + lead * jnp.where(toward, top_2, top),
                jnp.where(toward, bottom, bottom_2) + lead * jnp.where(toward, bottom_2, bottom),
                passing * passing_2,
            ))
        whole = joined
    top, bottom, passing = whole[0]
    out[:ROWS] = top
    out[ROWS:] = jnp.where(lower, bottom, 1.0 - passing)


def per_device(volume, knot_bins, colour_table, view_side):
    planes, tile_rows, columns = volume.shape
    slabs, tiles = lax.axis_size("slab"), lax.axis_size("tile")
    pieces = columns // LANES
    unit = 4 * pieces
    groups = ROWS // 2

    vmem = pl.BlockSpec(memory_space=pltpu.VMEM)
    hbm = pl.BlockSpec(memory_space=pltpu.HBM)
    small = pltpu.CompilerParams(vmem_limit_bytes=SMALL_VMEM)

    def array(*shape):
        return jax.ShapeDtypeStruct(shape, jnp.float32)

    inputs = (volume, knot_bins, colour_table, view_side.reshape(1, columns))
    inputs = [pltpu.with_memory_space_constraint(x, pltpu.HBM) for x in inputs]
    plane = pltpu.VMEM((1, tile_rows, columns), jnp.float32)
    row = pltpu.VMEM((planes, pieces, LANES), jnp.float32)
    pad, *edges, tables, side = pl.pallas_call(
        lambda *refs: load_kernel(planes * slabs, *refs),
        out_shape=[
            pltpu.VMEM((planes + 2, pieces * (tile_rows + 2 * ROWS), LANES), jnp.float32),
            plane, plane, row, row,
            pltpu.VMEM((9, ROWS, LANES), jnp.float32),
            pltpu.VMEM((1, columns), jnp.int32),
        ],
        in_specs=[hbm] * 4,
        out_specs=[vmem] * 7,
        scratch_shapes=[
            pltpu.SMEM((KNOTS,), jnp.int32),
            pltpu.SMEM((4, KNOTS), jnp.float32),
            pltpu.SemaphoreType.DMA((LOAD_PARTS * pieces,)),
            pltpu.SemaphoreType.DMA((3,)),
        ],
        compiler_params=small,
        name="load",
    )(*inputs)

    def swap(block, axis, size, low):
        route = [(i, i + 1) for i in range(low, size - 1, 2)]
        return lax.ppermute(block, axis, route + [(j, i) for i, j in route])

    halo = [
        swap(edges[0], "slab", slabs, 0),
        swap(edges[1], "slab", slabs, 1),
        swap(edges[2], "tile", tiles, 0),
        swap(edges[3], "tile", tiles, 1),
    ]

    def cost(steps):
        count = steps * ROWS * columns
        return pl.CostEstimate(flops=100 * count, bytes_accessed=16 * count, transcendentals=2 * count)

    inner = (ROWS - 3) * (planes - 2)
    outer = (ROWS * planes - inner) // 2
    stash = pltpu.VMEM((planes * pieces, ROWS, LANES), jnp.float32)
    states = pl.pallas_call(
        inner_kernel,
        out_shape=array(ROWS, 4, ROWS, columns),
        in_specs=[vmem] * 3,
        out_specs=vmem,
        scratch_shapes=[stash],
        compiler_params=small,
        cost_estimate=cost(inner),
        name="inner",
    )(pad, tables, side)

    def finish_sent(pad_in, near, far, row_near, row_far, states, tables, side, pad, out, stash):
        add_halo(pad, near, far, row_near, row_far)
        (core,) = low_bits("slab", 0)
        finish(pad, states, tables, side, out, stash, 1 - core, 1)

    def finish_kept(pad, states, tables, side, out, stash):
        (core,) = low_bits("slab", 0)
        finish(pad, states, tables, side, out, stash, core, 2)

    half = array(groups, 4, ROWS, columns)
    pad, sent = pl.pallas_call(
        finish_sent,
        out_shape=[array(*pad.shape), half],
        in_specs=[vmem] * 8,
        out_specs=[vmem] * 2,
        input_output_aliases={0: 0},
        scratch_shapes=[stash],
        compiler_params=small,
        cost_estimate=cost(outer),
        name="finish_sent",
    )(pad, *halo, states, tables, side)
    got = lax.ppermute(sent, "slab", [(i, i ^ 1) for i in range(slabs)])
    kept = pl.pallas_call(
        finish_kept,
        out_shape=half,
        in_specs=[vmem] * 4,
        out_specs=vmem,
        scratch_shapes=[stash],
        compiler_params=small,
        cost_estimate=cost(outer),
        name="finish_kept",
    )(pad, states, tables, side)

    def pair(mine, other, side_ref, out):
        (core,) = low_bits("slab", 0)
        for p in range(pieces):
            c = slice(p * LANES, (p + 1) * LANES)
            front = jnp.broadcast_to(side_ref[:, c], (ROWS, LANES)) + core == 1
            for x in range(groups):
                whole = merge(front, [mine[x, k, :, c] for k in range(4)], [other[x, k, :, c] for k in range(4)])
                for k, value in enumerate(whole):
                    out[pl.ds(x * unit + k * pieces + p, ROWS, stride=groups * unit), :] = value

    merged = pl.pallas_call(
        pair,
        out_shape=array(ROWS * groups * unit, LANES),
        in_specs=[vmem] * 3,
        out_specs=vmem,
        compiler_params=small,
        name="pair",
    )(kept, got, side)
    members = [[2 * q + c for q in range(slabs // 2)] for c in range(2)]
    parts = lax.all_to_all(
        merged.reshape(slabs // 2, unit, LANES), "slab", 0, 0, axis_index_groups=members, tiled=True
    )
    image = pl.pallas_call(
        final_kernel,
        out_shape=array(unit, LANES),
        in_specs=[vmem] * 2,
        out_specs=vmem,
        compiler_params=small,
        name="final",
    )(parts, side.reshape(pieces, LANES))
    return image.reshape(4, 1, 1, columns)


def solution(mesh):
    return jax.shard_map(
        per_device,
        mesh=mesh,
        in_specs=(P("slab", "tile", None), P(), P(), P()),
        out_specs=P(None, "slab", "tile", None),
        check_vma=False,
    )
```

```python
import jax
import jax.numpy as jnp
from jax import lax
from jax.experimental import pallas as pl
from jax.experimental.pallas import tpu as pltpu
from jax.sharding import PartitionSpec as P

BINS = 256
KNOTS = 8
LOG2_E = 1.4426950408889634
LANES = 128
ROWS = 8
SMALL_VMEM = 4 << 20
FACING = 0.7 * 0.64
LOAD_PARTS = 1
INNER_UNROLL = 5


def knot_tables(knot_bins, colour_table, total_planes):
    sublane = lax.broadcasted_iota(jnp.int32, (ROWS, LANES), 0)

    def spread(read):
        table = jnp.full((ROWS, LANES), read(0), jnp.float32)
        for knot in range(1, KNOTS):
            table = jnp.where(sublane == knot, read(knot), table)
        return table

    scale = 6.0 / (BINS - 1)
    knot_at = spread(lambda knot: knot_bins[knot].astype(jnp.float32)) * scale - 3.0
    knot_at = jnp.where(sublane == KNOTS - 1, 3.0, knot_at)
    width = pltpu.roll(knot_at, KNOTS - 1, 0) - knot_at
    starts, slopes = [], []
    for channel in range(4):
        start = spread(lambda knot: colour_table[channel, knot])
        rise = (pltpu.roll(start, KNOTS - 1, 0) - start) / width
        slope = jnp.where(sublane == KNOTS - 1, 0.0, rise)
        factor = -400.0 / total_planes * LOG2_E if channel == 3 else FACING
        starts.append(start * factor)
        slopes.append(slope * factor)
    return [knot_at] + starts + slopes


def look_up(value, tables, edges):
    index = jnp.zeros(value.shape, jnp.int32)
    for knot in range(1, KNOTS - 1):
        index = jnp.where(value >= edges[knot], knot, index)

    def pick(table):
        return jnp.take_along_axis(table, index, axis=0, mode="promise_in_bounds")

    offset = value - pick(tables[0])
    return [pick(tables[1 + c]) + offset * pick(tables[5 + c]) for c in range(4)]


def low_bits(axis, *bits):
    index = lax.axis_index(axis)
    return [(index >> bit) & 1 for bit in bits]


def load_kernel(
    total_planes, volume, knots_hbm, colours_hbm, side_hbm,
    pad, plane_near, plane_far, row_near, row_far, tables_ref, side_ref, knot_ref, colour_ref, sems, small_sems,
):
    planes, tile_rows, columns = volume.shape
    pieces = columns // LANES
    (core,), (tile,) = low_bits("slab", 0), low_bits("tile", 0)
    small = [
        pltpu.make_async_copy(knots_hbm, knot_ref, small_sems.at[0]),
        pltpu.make_async_copy(colours_hbm, colour_ref, small_sems.at[1]),
        pltpu.make_async_copy(side_hbm, side_ref, small_sems.at[2]),
    ]
    fetches = []
    share = planes // LOAD_PARTS
    for k in range(LOAD_PARTS):
        for p in range(pieces):
            source = volume.at[pl.ds(k * share, share), :, pl.ds(p * LANES, LANES)]
            target = pad.at[pl.ds(k * share + 1, share), pl.ds(pad_row(tile_rows, p, 0), tile_rows)]
            fetches.append(pltpu.make_async_copy(source, target, sems.at[k * pieces + p]))
    for copy in small + fetches:
        copy.start()
    for copy in small:
        copy.wait()
    for k, table in enumerate(knot_tables(knot_ref, colour_ref, total_planes)):
        tables_ref[k] = table
    for fetch in fetches:
        fetch.wait()
    stride = tile_rows + 2 * ROWS
    near, far = [pad_row(tile_rows, 0, 0) + (tile_rows - 1) * at for at in (1 - tile, tile)]
    for plane in range(planes):
        row_near[plane] = pad[plane + 1, pl.ds(near, pieces, stride=stride), :]
        row_far[plane] = pad[plane + 1, pl.ds(far, pieces, stride=stride), :]
    for p in range(pieces):
        rows = slice(pad_row(tile_rows, p, 0), pad_row(tile_rows, p, tile_rows))
        lanes = slice(p * LANES, (p + 1) * LANES)
        plane_near[0, :, lanes] = pad[1 + (planes - 1) * (1 - core), rows, :]
        plane_far[0, :, lanes] = pad[1 + (planes - 1) * core, rows, :]


def pad_row(tile_rows, piece, row):
    return piece * (tile_rows + 2 * ROWS) + ROWS + row


def at_end(axis):
    index = lax.axis_index(axis)
    return (index == 0) | (index == lax.axis_size(axis) - 1)


def add_halo(pad, plane_near, plane_far, row_near, row_far):
    _, tile_rows, columns = plane_near.shape
    planes, pieces, _ = row_near.shape
    (core,), (tile,) = low_bits("slab", 0), low_bits("tile", 0)
    for p in range(pieces):
        lanes = slice(p * LANES, (p + 1) * LANES)
        rows = slice(pad_row(tile_rows, p, 0), pad_row(tile_rows, p, tile_rows))
        pad[(planes + 1) * (1 - core), rows, :] = plane_near[0, :, lanes]
        pad[(planes + 1) * core, rows, :] = jnp.where(at_end("slab"), 0.0, plane_far[0, :, lanes])
    first, stride = pad_row(tile_rows, 0, -1), tile_rows + 2 * ROWS
    for plane in range(planes):
        pad[plane + 1, pl.ds(first + (tile_rows + 1) * (1 - tile), pieces, stride=stride), :] = row_near[plane]
        far = jnp.where(at_end("tile"), 0.0, row_far[plane])
        pad[plane + 1, pl.ds(first + (tile_rows + 1) * tile, pieces, stride=stride), :] = far


class Marcher:
    def __init__(self, pad, tables_ref, side_ref, stash):
        self.pad, self.stash = pad, stash
        self.pieces = side_ref.shape[1] // LANES
        self.planes = pad.shape[0] - 2
        self.tables = [tables_ref[k] for k in range(tables_ref.shape[0])]
        at = self.tables[0]
        self.edges = [jnp.broadcast_to(at[k : k + 1], (ROWS, LANES)) for k in range(KNOTS)]
        self.lane = lax.broadcasted_iota(jnp.int32, (ROWS, LANES), 1)
        self.lanes = [slice(p * LANES, (p + 1) * LANES) for p in range(self.pieces)]
        self.toward = [jnp.broadcast_to(side_ref[:, c], (ROWS, LANES)) == 1 for c in self.lanes]

    def read(self, group, plane, piece, shift=0):
        row = pad_row(ROWS * ROWS, piece, group + shift)
        return self.pad[plane + 1, pl.ds(row, ROWS, stride=ROWS), :]

    def start(self):
        zero = jnp.zeros((ROWS, LANES), jnp.float32)
        return [[zero] * self.pieces for _ in range(3)] + [[zero + 1.0] * self.pieces]

    def load(self, ref):
        return [[ref[k, :, c] for c in self.lanes] for k in range(4)]

    def store(self, ref, state):
        for k in range(4):
            for p, c in enumerate(self.lanes):
                ref[k, :, c] = state[k][p]

    def shade(self, group, plane, held):
        lane, zero = self.lane, jnp.zeros((ROWS, LANES), jnp.float32)
        for q in range(plane - 1, plane + 2):
            if q not in held:
                held[q] = [self.read(group, q, p) for p in range(self.pieces)]
        before, here, after = [held[plane + d] for d in (-1, 0, 1)]
        to_left = [pltpu.roll(v, LANES - 1, 1) for v in here] + [zero]
        to_right = [zero] + [pltpu.roll(v, 1, 1) for v in here]
        strengths = []
        for p in range(self.pieces):
            depth = after[p] - before[p]
            rows = self.read(group, plane, p, 1) - self.read(group, plane, p, -1)
            col_up = jnp.where(lane == 0, to_right[p], to_right[p + 1])
            col_down = jnp.where(lane == LANES - 1, to_left[p + 1], to_left[p])
            across = col_down - col_up
            facing = jnp.abs(depth + (0.6 / 0.64) * rows + (0.48 / 0.64) * across)
            square = depth * depth + rows * rows + (across * across + 4.0)
            strengths.append(0.3 / FACING + facing * lax.rsqrt(square))
        return here, strengths

    def pair(self, group, plane, held):
        (low, low_strength), (high, high_strength) = [
            self.shade(group, q, held) for q in (plane, self.planes - 1 - plane)
        ]
        near, far = [], []
        for p, toward in enumerate(self.toward):
            near.append((jnp.where(toward, low[p], high[p]), jnp.where(toward, low_strength[p], high_strength[p])))
            far.append((jnp.where(toward, high[p], low[p]), jnp.where(toward, high_strength[p], low_strength[p])))
        return near, far

    def behind(self, state, plane):
        new = [[], [], [], []]
        for p, (x, strength) in enumerate(plane):
            clipped = jnp.minimum(jnp.maximum(x, -3.0), 3.0)
            red, green, blue, exponent = look_up(clipped, self.tables, self.edges)
            left = state[3][p] * jnp.exp2(exponent)
            weight = (state[3][p] - left) * strength
            for channel, value in enumerate((red, green, blue)):
                new[channel].append(state[channel][p] + weight * value)
            new[3].append(left)
        return new

    def run(self, group, first):
        state, held = self.start(), {}
        for plane in range(first, self.planes // 2):
            near, far = self.pair(group, plane, held)
            state = self.behind(state, near)
            for p in range(self.pieces):
                for k in range(2):
                    self.stash[(plane * self.pieces + p) * 2 + k] = far[p][k]
        for plane in reversed(range(first, self.planes // 2)):
            at = [(plane * self.pieces + p) * 2 for p in range(self.pieces)]
            state = self.behind(state, [(self.stash[k], self.stash[k + 1]) for k in at])
        return state

    def ends(self, state, group):
        near, far = self.pair(group, 0, {})
        front = self.behind(self.start(), near)
        state = [
            [front[k][p] + front[3][p] * state[k][p] if k < 3 else front[3][p] * state[3][p] for p in range(self.pieces)]
            for k in range(4)
        ]
        return self.behind(state, far)


def late_group(parity):
    return ROWS - 2 - parity


def inner_kernel(pad, tables_ref, side_ref, states, stash):
    marcher = Marcher(pad, tables_ref, side_ref, stash)
    (core,) = low_bits("slab", 0)

    def group(j, carry):
        g = 1 + j + (1 + j >= late_group(core)).astype(jnp.int32)
        marcher.store(states.at[g], marcher.run(g, 1))
        return carry

    lax.fori_loop(0, ROWS - 3, group, 0, unroll=INNER_UNROLL)


def finish(pad, states, tables_ref, side_ref, out, stash, parity, left):
    marcher = Marcher(pad, tables_ref, side_ref, stash)

    def whole(t, carry):
        g = jnp.where(t == 0, parity * (ROWS - 1), late_group(parity))
        marcher.store(out.at[g >> 1], marcher.run(g, 0))
        return carry

    def group(j, carry):
        g = 2 - parity + 2 * j
        marcher.store(out.at[g >> 1], marcher.ends(marcher.load(states.at[g]), g))
        return carry

    lax.fori_loop(0, left, whole, 0, unroll=True)
    lax.fori_loop(0, ROWS // 2 - left, group, 0, unroll=True)


def merge(first_is_front, mine, other):
    lead = jnp.where(first_is_front, mine[3], other[3])
    merged = [
        jnp.where(first_is_front, mine[c], other[c]) + lead * jnp.where(first_is_front, other[c], mine[c])
        for c in range(3)
    ]
    return merged + [mine[3] * other[3]]


def both_halves(value):
    sublane = lax.broadcasted_iota(jnp.int32, value.shape, 0)
    return jnp.where(sublane < 4, pltpu.roll(value, 4, 0), value)


def final_kernel(parts, side_ref, out):
    toward = jnp.concatenate([side_ref[...]] * 2, axis=0) == 1
    lower = lax.broadcasted_iota(jnp.int32, (ROWS, LANES), 0) < 4
    whole = [(parts[k, :ROWS], parts[k, ROWS:], both_halves(parts[k, ROWS:])) for k in range(parts.shape[0])]
    while len(whole) > 1:
        joined = []
        for (top, bottom, passing), (top_2, bottom_2, passing_2) in zip(whole[::2], whole[1::2]):
            lead = jnp.where(toward, passing, passing_2)
            joined.append((
                jnp.where(toward, top, top_2) + lead * jnp.where(toward, top_2, top),
                jnp.where(toward, bottom, bottom_2) + lead * jnp.where(toward, bottom_2, bottom),
                passing * passing_2,
            ))
        whole = joined
    top, bottom, passing = whole[0]
    out[:ROWS] = top
    out[ROWS:] = jnp.where(lower, bottom, 1.0 - passing)


def per_device(volume, knot_bins, colour_table, view_side):
    planes, tile_rows, columns = volume.shape
    slabs, tiles = lax.axis_size("slab"), lax.axis_size("tile")
    pieces = columns // LANES
    unit = 4 * pieces
    groups = ROWS // 2

    vmem = pl.BlockSpec(memory_space=pltpu.VMEM)
    hbm = pl.BlockSpec(memory_space=pltpu.HBM)
    small = pltpu.CompilerParams(vmem_limit_bytes=SMALL_VMEM)

    def array(*shape):
        return jax.ShapeDtypeStruct(shape, jnp.float32)

    inputs = (volume, knot_bins, colour_table, view_side.reshape(1, columns))
    inputs = [pltpu.with_memory_space_constraint(x, pltpu.HBM) for x in inputs]
    plane = pltpu.VMEM((1, tile_rows, columns), jnp.float32)
    row = pltpu.VMEM((planes, pieces, LANES), jnp.float32)
    pad, *edges, tables, side = pl.pallas_call(
        lambda *refs: load_kernel(planes * slabs, *refs),
        out_shape=[
            pltpu.VMEM((planes + 2, pieces * (tile_rows + 2 * ROWS), LANES), jnp.float32),
            plane, plane, row, row,
            pltpu.VMEM((9, ROWS, LANES), jnp.float32),
            pltpu.VMEM((1, columns), jnp.int32),
        ],
        in_specs=[hbm] * 4,
        out_specs=[vmem] * 7,
        scratch_shapes=[
            pltpu.SMEM((KNOTS,), jnp.int32),
            pltpu.SMEM((4, KNOTS), jnp.float32),
            pltpu.SemaphoreType.DMA((LOAD_PARTS * pieces,)),
            pltpu.SemaphoreType.DMA((3,)),
        ],
        compiler_params=small,
        name="load",
    )(*inputs)

    def swap(block, axis, size, low):
        route = [(i, (i + 1) % size) for i in range(low, size, 2)]
        return lax.ppermute(block, axis, route + [(j, i) for i, j in route])

    halo = [
        swap(edges[0], "slab", slabs, 0),
        swap(edges[1], "slab", slabs, 1),
        swap(edges[2], "tile", tiles, 0),
        swap(edges[3], "tile", tiles, 1),
    ]

    def cost(steps):
        count = steps * ROWS * columns
        return pl.CostEstimate(flops=100 * count, bytes_accessed=16 * count, transcendentals=2 * count)

    inner = (ROWS - 3) * (planes - 2)
    outer = (ROWS * planes - inner) // 2
    stash = pltpu.VMEM((planes * pieces, ROWS, LANES), jnp.float32)
    states = pl.pallas_call(
        inner_kernel,
        out_shape=array(ROWS, 4, ROWS, columns),
        in_specs=[vmem] * 3,
        out_specs=vmem,
        scratch_shapes=[stash],
        compiler_params=small,
        cost_estimate=cost(inner),
        name="inner",
    )(pad, tables, side)

    def finish_sent(pad_in, near, far, row_near, row_far, states, tables, side, pad, out, stash):
        add_halo(pad, near, far, row_near, row_far)
        (core,) = low_bits("slab", 0)
        finish(pad, states, tables, side, out, stash, 1 - core, 1)

    def finish_kept(pad, states, tables, side, out, stash):
        (core,) = low_bits("slab", 0)
        finish(pad, states, tables, side, out, stash, core, 2)

    half = array(groups, 4, ROWS, columns)
    pad, sent = pl.pallas_call(
        finish_sent,
        out_shape=[array(*pad.shape), half],
        in_specs=[vmem] * 8,
        out_specs=[vmem] * 2,
        input_output_aliases={0: 0},
        scratch_shapes=[stash],
        compiler_params=small,
        cost_estimate=cost(outer),
        name="finish_sent",
    )(pad, *halo, states, tables, side)
    got = lax.ppermute(sent, "slab", [(i, i ^ 1) for i in range(slabs)])
    kept = pl.pallas_call(
        finish_kept,
        out_shape=half,
        in_specs=[vmem] * 4,
        out_specs=vmem,
        scratch_shapes=[stash],
        compiler_params=small,
        cost_estimate=cost(outer),
        name="finish_kept",
    )(pad, states, tables, side)

    def pair(mine, other, side_ref, out):
        (core,) = low_bits("slab", 0)
        for p in range(pieces):
            c = slice(p * LANES, (p + 1) * LANES)
            front = jnp.broadcast_to(side_ref[:, c], (ROWS, LANES)) + core == 1
            for x in range(groups):
                whole = merge(front, [mine[x, k, :, c] for k in range(4)], [other[x, k, :, c] for k in range(4)])
                for k, value in enumerate(whole):
                    out[pl.ds(x * unit + k * pieces + p, ROWS, stride=groups * unit), :] = value

    merged = pl.pallas_call(
        pair,
        out_shape=array(ROWS * groups * unit, LANES),
        in_specs=[vmem] * 3,
        out_specs=vmem,
        compiler_params=small,
        name="pair",
    )(kept, got, side)
    members = [[2 * q + c for q in range(slabs // 2)] for c in range(2)]
    parts = lax.all_to_all(
        merged.reshape(slabs // 2, unit, LANES), "slab", 0, 0, axis_index_groups=members, tiled=True
    )
    image = pl.pallas_call(
        final_kernel,
        out_shape=array(unit, LANES),
        in_specs=[vmem] * 2,
        out_specs=vmem,
        compiler_params=small,
        name="final",
    )(parts, side.reshape(pieces, LANES))
    return image.reshape(4, 1, 1, columns)


def solution(mesh):
    return jax.shard_map(
        per_device,
        mesh=mesh,
        in_specs=(P("slab", "tile", None), P(), P(), P()),
        out_specs=P(None, "slab", "tile", None),
        check_vma=False,
    )
```

```python
import jax
import jax.numpy as jnp
from jax import lax
from jax.experimental import pallas as pl
from jax.experimental.pallas import tpu as pltpu
from jax.sharding import PartitionSpec as P

BINS = 256
KNOTS = 8
LOG2_E = 1.4426950408889634
LANES = 128
ROWS = 8
SMALL_VMEM = 4 << 20
FACING = 0.7 * 0.64
LOAD_PARTS = 1
INNER_UNROLL = 5


def knot_tables(knot_bins, colour_table, total_planes):
    sublane = lax.broadcasted_iota(jnp.int32, (ROWS, LANES), 0)

    def spread(read):
        table = jnp.full((ROWS, LANES), read(0), jnp.float32)
        for knot in range(1, KNOTS):
            table = jnp.where(sublane == knot, read(knot), table)
        return table

    scale = 6.0 / (BINS - 1)
    knot_at = spread(lambda knot: knot_bins[knot].astype(jnp.float32)) * scale - 3.0
    knot_at = jnp.where(sublane == KNOTS - 1, 3.0, knot_at)
    width = pltpu.roll(knot_at, KNOTS - 1, 0) - knot_at
    starts, slopes = [], []
    for channel in range(4):
        start = spread(lambda knot: colour_table[channel, knot])
        rise = (pltpu.roll(start, KNOTS - 1, 0) - start) / width
        slope = jnp.where(sublane == KNOTS - 1, 0.0, rise)
        factor = -400.0 / total_planes * LOG2_E if channel == 3 else FACING
        starts.append(start * factor)
        slopes.append(slope * factor)
    return [knot_at] + starts + slopes


def look_up(value, tables, edges):
    index = jnp.zeros(value.shape, jnp.int32)
    for knot in range(1, KNOTS - 1):
        index = jnp.where(value >= edges[knot], knot, index)

    def pick(table):
        return jnp.take_along_axis(table, index, axis=0, mode="promise_in_bounds")

    offset = value - pick(tables[0])
    return [pick(tables[1 + c]) + offset * pick(tables[5 + c]) for c in range(4)]


def low_bits(axis, *bits):
    index = lax.axis_index(axis)
    return [(index >> bit) & 1 for bit in bits]


def load_kernel(
    total_planes, volume, knots_hbm, colours_hbm, side_hbm,
    pad, plane_near, plane_far, row_near, row_far, tables_ref, side_ref, knot_ref, colour_ref, sems, small_sems,
):
    planes, tile_rows, columns = volume.shape
    pieces = columns // LANES
    (core,), (tile,) = low_bits("slab", 0), low_bits("tile", 0)
    small = [
        pltpu.make_async_copy(knots_hbm, knot_ref, small_sems.at[0]),
        pltpu.make_async_copy(colours_hbm, colour_ref, small_sems.at[1]),
        pltpu.make_async_copy(side_hbm, side_ref, small_sems.at[2]),
    ]
    fetches = []
    share = planes // LOAD_PARTS
    for k in range(LOAD_PARTS):
        for p in range(pieces):
            source = volume.at[pl.ds(k * share, share), :, pl.ds(p * LANES, LANES)]
            target = pad.at[pl.ds(k * share + 1, share), pl.ds(pad_row(tile_rows, p, 0), tile_rows)]
            fetches.append(pltpu.make_async_copy(source, target, sems.at[k * pieces + p]))
    for copy in small + fetches:
        copy.start()
    for copy in small:
        copy.wait()
    for k, table in enumerate(knot_tables(knot_ref, colour_ref, total_planes)):
        tables_ref[k] = table
    for fetch in fetches:
        fetch.wait()
    stride = tile_rows + 2 * ROWS
    near, far = [pad_row(tile_rows, 0, 0) + (tile_rows - 1) * at for at in (1 - tile, tile)]
    for plane in range(planes):
        row_near[plane] = pad[plane + 1, pl.ds(near, pieces, stride=stride), :]
        row_far[plane] = pad[plane + 1, pl.ds(far, pieces, stride=stride), :]
    for p in range(pieces):
        rows = slice(pad_row(tile_rows, p, 0), pad_row(tile_rows, p, tile_rows))
        lanes = slice(p * LANES, (p + 1) * LANES)
        plane_near[0, :, lanes] = pad[1 + (planes - 1) * (1 - core), rows, :]
        plane_far[0, :, lanes] = pad[1 + (planes - 1) * core, rows, :]


def pad_row(tile_rows, piece, row):
    return piece * (tile_rows + 2 * ROWS) + ROWS + row


def at_end(axis):
    index = lax.axis_index(axis)
    return (index == 0) | (index == lax.axis_size(axis) - 1)


def add_halo(pad, plane_near, plane_far, row_near, row_far):
    _, tile_rows, columns = plane_near.shape
    planes, pieces, _ = row_near.shape
    (core,), (tile,) = low_bits("slab", 0), low_bits("tile", 0)
    for p in range(pieces):
        lanes = slice(p * LANES, (p + 1) * LANES)
        rows = slice(pad_row(tile_rows, p, 0), pad_row(tile_rows, p, tile_rows))
        pad[(planes + 1) * (1 - core), rows, :] = plane_near[0, :, lanes]
        pad[(planes + 1) * core, rows, :] = jnp.where(at_end("slab"), 0.0, plane_far[0, :, lanes])
    first, stride = pad_row(tile_rows, 0, -1), tile_rows + 2 * ROWS
    for plane in range(planes):
        pad[plane + 1, pl.ds(first + (tile_rows + 1) * (1 - tile), pieces, stride=stride), :] = row_near[plane]
        far = jnp.where(at_end("tile"), 0.0, row_far[plane])
        pad[plane + 1, pl.ds(first + (tile_rows + 1) * tile, pieces, stride=stride), :] = far


class Marcher:
    def __init__(self, pad, tables_ref, side_ref, stash):
        self.pad, self.stash = pad, stash
        self.pieces = side_ref.shape[1] // LANES
        self.planes = pad.shape[0] - 2
        self.tables = [tables_ref[k] for k in range(tables_ref.shape[0])]
        at = self.tables[0]
        self.edges = [jnp.broadcast_to(at[k : k + 1], (ROWS, LANES)) for k in range(KNOTS)]
        self.lane = lax.broadcasted_iota(jnp.int32, (ROWS, LANES), 1)
        self.lanes = [slice(p * LANES, (p + 1) * LANES) for p in range(self.pieces)]
        self.toward = [jnp.broadcast_to(side_ref[:, c], (ROWS, LANES)) == 1 for c in self.lanes]

    def read(self, group, plane, piece, shift=0):
        row = pad_row(ROWS * ROWS, piece, group + shift)
        return self.pad[plane + 1, pl.ds(row, ROWS, stride=ROWS), :]

    def start(self):
        zero = jnp.zeros((ROWS, LANES), jnp.float32)
        return [[zero] * self.pieces for _ in range(3)] + [[zero + 1.0] * self.pieces]

    def load(self, ref):
        return [[ref[k, :, c] for c in self.lanes] for k in range(4)]

    def store(self, ref, state):
        for k in range(4):
            for p, c in enumerate(self.lanes):
                ref[k, :, c] = state[k][p]

    def shade(self, group, plane, held):
        lane, zero = self.lane, jnp.zeros((ROWS, LANES), jnp.float32)
        for q in range(plane - 1, plane + 2):
            if q not in held:
                held[q] = [self.read(group, q, p) for p in range(self.pieces)]
        before, here, after = [held[plane + d] for d in (-1, 0, 1)]
        to_left = [pltpu.roll(v, LANES - 1, 1) for v in here] + [zero]
        to_right = [zero] + [pltpu.roll(v, 1, 1) for v in here]
        strengths = []
        for p in range(self.pieces):
            depth = after[p] - before[p]
            rows = self.read(group, plane, p, 1) - self.read(group, plane, p, -1)
            col_up = jnp.where(lane == 0, to_right[p], to_right[p + 1])
            col_down = jnp.where(lane == LANES - 1, to_left[p + 1], to_left[p])
            across = col_down - col_up
            facing = jnp.abs(depth + (0.6 / 0.64) * rows + (0.48 / 0.64) * across)
            square = depth * depth + rows * rows + (across * across + 4.0)
            strengths.append(0.3 / FACING + facing * lax.rsqrt(square))
        return here, strengths

    def pair(self, group, plane, held):
        (low, low_strength), (high, high_strength) = [
            self.shade(group, q, held) for q in (plane, self.planes - 1 - plane)
        ]
        near, far = [], []
        for p, toward in enumerate(self.toward):
            near.append((jnp.where(toward, low[p], high[p]), jnp.where(toward, low_strength[p], high_strength[p])))
            far.append((jnp.where(toward, high[p], low[p]), jnp.where(toward, high_strength[p], low_strength[p])))
        return near, far

    def behind(self, state, plane):
        new = [[], [], [], []]
        for p, (x, strength) in enumerate(plane):
            clipped = jnp.minimum(jnp.maximum(x, -3.0), 3.0)
            red, green, blue, exponent = look_up(clipped, self.tables, self.edges)
            left = state[3][p] * jnp.exp2(exponent)
            weight = (state[3][p] - left) * strength
            for channel, value in enumerate((red, green, blue)):
                new[channel].append(state[channel][p] + weight * value)
            new[3].append(left)
        return new

    def run(self, group, first):
        state, held = self.start(), {}
        for plane in range(first, self.planes // 2):
            near, far = self.pair(group, plane, held)
            state = self.behind(state, near)
            for p in range(self.pieces):
                for k in range(2):
                    self.stash[(plane * self.pieces + p) * 2 + k] = far[p][k]
        for plane in reversed(range(first, self.planes // 2)):
            at = [(plane * self.pieces + p) * 2 for p in range(self.pieces)]
            state = self.behind(state, [(self.stash[k], self.stash[k + 1]) for k in at])
        return state

    def ends(self, state, group):
        near, far = self.pair(group, 0, {})
        front = self.behind(self.start(), near)
        state = [
            [front[k][p] + front[3][p] * state[k][p] if k < 3 else front[3][p] * state[3][p] for p in range(self.pieces)]
            for k in range(4)
        ]
        return self.behind(state, far)


def late_group(parity):
    return ROWS - 2 - parity


def inner_kernel(pad, tables_ref, side_ref, states, stash):
    marcher = Marcher(pad, tables_ref, side_ref, stash)
    (core,) = low_bits("slab", 0)

    def group(j, carry):
        g = 1 + j + (1 + j >= late_group(core)).astype(jnp.int32)
        marcher.store(states.at[g], marcher.run(g, 1))
        return carry

    lax.fori_loop(0, ROWS - 3, group, 0, unroll=INNER_UNROLL)


def finish(pad, states, tables_ref, side_ref, out, stash, parity, left):
    marcher = Marcher(pad, tables_ref, side_ref, stash)

    def whole(t, carry):
        g = jnp.where(t == 0, parity * (ROWS - 1), late_group(parity))
        marcher.store(out.at[g >> 1], marcher.run(g, 0))
        return carry

    def group(j, carry):
        g = 2 - parity + 2 * j
        marcher.store(out.at[g >> 1], marcher.ends(marcher.load(states.at[g]), g))
        return carry

    lax.fori_loop(0, left, whole, 0, unroll=True)
    lax.fori_loop(0, ROWS // 2 - left, group, 0, unroll=True)


def merge(first_is_front, mine, other):
    lead = jnp.where(first_is_front, mine[3], other[3])
    merged = [
        jnp.where(first_is_front, mine[c], other[c]) + lead * jnp.where(first_is_front, other[c], mine[c])
        for c in range(3)
    ]
    return merged + [mine[3] * other[3]]


def both_halves(value):
    sublane = lax.broadcasted_iota(jnp.int32, value.shape, 0)
    return jnp.where(sublane < 4, pltpu.roll(value, 4, 0), value)


def final_kernel(parts, side_ref, out):
    toward = jnp.concatenate([side_ref[...]] * 2, axis=0) == 1
    lower = lax.broadcasted_iota(jnp.int32, (ROWS, LANES), 0) < 4
    whole = [(parts[k, :ROWS], parts[k, ROWS:], both_halves(parts[k, ROWS:])) for k in range(parts.shape[0])]
    while len(whole) > 1:
        joined = []
        for (top, bottom, passing), (top_2, bottom_2, passing_2) in zip(whole[::2], whole[1::2]):
            lead = jnp.where(toward, passing, passing_2)
            joined.append((
                jnp.where(toward, top, top_2) + lead * jnp.where(toward, top_2, top),
                jnp.where(toward, bottom, bottom_2) + lead * jnp.where(toward, bottom_2, bottom),
                passing * passing_2,
            ))
        whole = joined
    top, bottom, passing = whole[0]
    out[:ROWS] = top
    out[ROWS:] = jnp.where(lower, bottom, 1.0 - passing)


def per_device(volume, knot_bins, colour_table, view_side):
    planes, tile_rows, columns = volume.shape
    slabs, tiles = lax.axis_size("slab"), lax.axis_size("tile")
    pieces = columns // LANES
    unit = 4 * pieces
    groups = ROWS // 2

    vmem = pl.BlockSpec(memory_space=pltpu.VMEM)
    hbm = pl.BlockSpec(memory_space=pltpu.HBM)
    small = pltpu.CompilerParams(vmem_limit_bytes=SMALL_VMEM)

    def array(*shape):
        return jax.ShapeDtypeStruct(shape, jnp.float32)

    inputs = (volume, knot_bins, colour_table, view_side.reshape(1, columns))
    inputs = [pltpu.with_memory_space_constraint(x, pltpu.HBM) for x in inputs]
    plane = pltpu.VMEM((1, tile_rows, columns), jnp.float32)
    row = pltpu.VMEM((planes, pieces, LANES), jnp.float32)
    pad, *edges, tables, side = pl.pallas_call(
        lambda *refs: load_kernel(planes * slabs, *refs),
        out_shape=[
            pltpu.VMEM((planes + 2, pieces * (tile_rows + 2 * ROWS), LANES), jnp.float32),
            plane, plane, row, row,
            pltpu.VMEM((9, ROWS, LANES), jnp.float32),
            pltpu.VMEM((1, columns), jnp.int32),
        ],
        in_specs=[hbm] * 4,
        out_specs=[vmem] * 7,
        scratch_shapes=[
            pltpu.SMEM((KNOTS,), jnp.int32),
            pltpu.SMEM((4, KNOTS), jnp.float32),
            pltpu.SemaphoreType.DMA((LOAD_PARTS * pieces,)),
            pltpu.SemaphoreType.DMA((3,)),
        ],
        compiler_params=small,
        name="load",
    )(*inputs)

    def swap(block, axis, low):
        route = []
        for slab in range(slabs):
            for tile in range(tiles):
                index, size = (slab, slabs) if axis == "slab" else (tile, tiles)
                step = 1 if (index - low) % 2 == 0 else -1
                if not 0 <= index + step < size:
                    other = (slab, tile ^ 1) if axis == "slab" else (slab ^ 1, tile)
                else:
                    other = (slab + step, tile) if axis == "slab" else (slab, tile + step)
                route.append((slab * tiles + tile, other[0] * tiles + other[1]))
        return lax.ppermute(block, ("slab", "tile"), route)

    halo = [
        swap(edges[0], "slab", 0),
        swap(edges[1], "slab", 1),
        swap(edges[2], "tile", 0),
        swap(edges[3], "tile", 1),
    ]

    def cost(steps):
        count = steps * ROWS * columns
        return pl.CostEstimate(flops=100 * count, bytes_accessed=16 * count, transcendentals=2 * count)

    inner = (ROWS - 3) * (planes - 2)
    outer = (ROWS * planes - inner) // 2
    stash = pltpu.VMEM((planes * pieces, ROWS, LANES), jnp.float32)
    states = pl.pallas_call(
        inner_kernel,
        out_shape=array(ROWS, 4, ROWS, columns),
        in_specs=[vmem] * 3,
        out_specs=vmem,
        scratch_shapes=[stash],
        compiler_params=small,
        cost_estimate=cost(inner),
        name="inner",
    )(pad, tables, side)

    def finish_sent(pad_in, near, far, row_near, row_far, states, tables, side, pad, out, stash):
        add_halo(pad, near, far, row_near, row_far)
        (core,) = low_bits("slab", 0)
        finish(pad, states, tables, side, out, stash, 1 - core, 1)

    def finish_kept(pad, states, tables, side, out, stash):
        (core,) = low_bits("slab", 0)
        finish(pad, states, tables, side, out, stash, core, 2)

    half = array(groups, 4, ROWS, columns)
    pad, sent = pl.pallas_call(
        finish_sent,
        out_shape=[array(*pad.shape), half],
        in_specs=[vmem] * 8,
        out_specs=[vmem] * 2,
        input_output_aliases={0: 0},
        scratch_shapes=[stash],
        compiler_params=small,
        cost_estimate=cost(outer),
        name="finish_sent",
    )(pad, *halo, states, tables, side)
    got = lax.ppermute(sent, "slab", [(i, i ^ 1) for i in range(slabs)])
    kept = pl.pallas_call(
        finish_kept,
        out_shape=half,
        in_specs=[vmem] * 4,
        out_specs=vmem,
        scratch_shapes=[stash],
        compiler_params=small,
        cost_estimate=cost(outer),
        name="finish_kept",
    )(pad, states, tables, side)

    def pair(mine, other, side_ref, out):
        (core,) = low_bits("slab", 0)
        for p in range(pieces):
            c = slice(p * LANES, (p + 1) * LANES)
            front = jnp.broadcast_to(side_ref[:, c], (ROWS, LANES)) + core == 1
            for x in range(groups):
                whole = merge(front, [mine[x, k, :, c] for k in range(4)], [other[x, k, :, c] for k in range(4)])
                for k, value in enumerate(whole):
                    out[pl.ds(x * unit + k * pieces + p, ROWS, stride=groups * unit), :] = value

    merged = pl.pallas_call(
        pair,
        out_shape=array(ROWS * groups * unit, LANES),
        in_specs=[vmem] * 3,
        out_specs=vmem,
        compiler_params=small,
        name="pair",
    )(kept, got, side)
    members = [[2 * q + c for q in range(slabs // 2)] for c in range(2)]
    parts = lax.all_to_all(
        merged.reshape(slabs // 2, unit, LANES), "slab", 0, 0, axis_index_groups=members, tiled=True
    )
    image = pl.pallas_call(
        final_kernel,
        out_shape=array(unit, LANES),
        in_specs=[vmem] * 2,
        out_specs=vmem,
        compiler_params=small,
        name="final",
    )(parts, side.reshape(pieces, LANES))
    return image.reshape(4, 1, 1, columns)


def solution(mesh):
    return jax.shard_map(
        per_device,
        mesh=mesh,
        in_specs=(P("slab", "tile", None), P(), P(), P()),
        out_specs=P(None, "slab", "tile", None),
        check_vma=False,
    )
```

```python
import jax
import jax.numpy as jnp
from jax import lax
from jax.experimental import pallas as pl
from jax.experimental.pallas import tpu as pltpu
from jax.sharding import PartitionSpec as P

BINS = 256
KNOTS = 8
LOG2_E = 1.4426950408889634
LANES = 128
ROWS = 8
SMALL_VMEM = 4 << 20
FACING = 0.7 * 0.64
LOAD_PARTS = 1
INNER_UNROLL = 5


def knot_tables(knot_bins, colour_table, total_planes):
    sublane = lax.broadcasted_iota(jnp.int32, (ROWS, LANES), 0)

    def spread(read):
        table = jnp.full((ROWS, LANES), read(0), jnp.float32)
        for knot in range(1, KNOTS):
            table = jnp.where(sublane == knot, read(knot), table)
        return table

    scale = 6.0 / (BINS - 1)
    knot_at = spread(lambda knot: knot_bins[knot].astype(jnp.float32)) * scale - 3.0
    knot_at = jnp.where(sublane == KNOTS - 1, 3.0, knot_at)
    width = pltpu.roll(knot_at, KNOTS - 1, 0) - knot_at
    starts, slopes = [], []
    for channel in range(4):
        start = spread(lambda knot: colour_table[channel, knot])
        rise = (pltpu.roll(start, KNOTS - 1, 0) - start) / width
        slope = jnp.where(sublane == KNOTS - 1, 0.0, rise)
        factor = -400.0 / total_planes * LOG2_E if channel == 3 else FACING
        starts.append(start * factor)
        slopes.append(slope * factor)
    return [knot_at] + starts + slopes


def look_up(value, tables, edges):
    index = jnp.zeros(value.shape, jnp.int32)
    for knot in range(1, KNOTS - 1):
        index = jnp.where(value >= edges[knot], knot, index)

    def pick(table):
        return jnp.take_along_axis(table, index, axis=0, mode="promise_in_bounds")

    offset = value - pick(tables[0])
    return [pick(tables[1 + c]) + offset * pick(tables[5 + c]) for c in range(4)]


def low_bits(axis, *bits):
    index = lax.axis_index(axis)
    return [(index >> bit) & 1 for bit in bits]


def load_kernel(
    total_planes, volume, knots_hbm, colours_hbm, side_hbm,
    pad, plane_near, plane_far, row_near, row_far, tables_ref, side_ref, knot_ref, colour_ref, sems, small_sems,
):
    planes, tile_rows, columns = volume.shape
    pieces = columns // LANES
    (core,), (tile,) = low_bits("slab", 0), low_bits("tile", 0)
    small = [
        pltpu.make_async_copy(knots_hbm, knot_ref, small_sems.at[0]),
        pltpu.make_async_copy(colours_hbm, colour_ref, small_sems.at[1]),
        pltpu.make_async_copy(side_hbm, side_ref, small_sems.at[2]),
    ]
    fetches = []
    share = planes // LOAD_PARTS
    for k in range(LOAD_PARTS):
        for p in range(pieces):
            source = volume.at[pl.ds(k * share, share), :, pl.ds(p * LANES, LANES)]
            target = pad.at[pl.ds(k * share + 1, share), pl.ds(pad_row(tile_rows, p, 0), tile_rows)]
            fetches.append(pltpu.make_async_copy(source, target, sems.at[k * pieces + p]))
    for copy in small + fetches:
        copy.start()
    for copy in small:
        copy.wait()
    for k, table in enumerate(knot_tables(knot_ref, colour_ref, total_planes)):
        tables_ref[k] = table
    for fetch in fetches:
        fetch.wait()
    stride = tile_rows + 2 * ROWS
    near, far = [pad_row(tile_rows, 0, 0) + (tile_rows - 1) * at for at in (1 - tile, tile)]
    for plane in range(planes):
        row_near[plane] = pad[plane + 1, pl.ds(near, pieces, stride=stride), :]
        row_far[plane] = pad[plane + 1, pl.ds(far, pieces, stride=stride), :]
    for p in range(pieces):
        rows = slice(pad_row(tile_rows, p, 0), pad_row(tile_rows, p, tile_rows))
        lanes = slice(p * LANES, (p + 1) * LANES)
        plane_near[0, :, lanes] = pad[1 + (planes - 1) * (1 - core), rows, :]
        plane_far[0, :, lanes] = pad[1 + (planes - 1) * core, rows, :]


def pad_row(tile_rows, piece, row):
    return piece * (tile_rows + 2 * ROWS) + ROWS + row


def at_end(axis):
    index = lax.axis_index(axis)
    return (index == 0) | (index == lax.axis_size(axis) - 1)


def add_halo(pad, plane_near, plane_far, row_near, row_far):
    _, tile_rows, columns = plane_near.shape
    planes, pieces, _ = row_near.shape
    (core,), (tile,) = low_bits("slab", 0), low_bits("tile", 0)
    for p in range(pieces):
        lanes = slice(p * LANES, (p + 1) * LANES)
        rows = slice(pad_row(tile_rows, p, 0), pad_row(tile_rows, p, tile_rows))
        pad[(planes + 1) * (1 - core), rows, :] = plane_near[0, :, lanes]
        pad[(planes + 1) * core, rows, :] = jnp.where(at_end("slab"), 0.0, plane_far[0, :, lanes])
    first, stride = pad_row(tile_rows, 0, -1), tile_rows + 2 * ROWS
    for plane in range(planes):
        pad[plane + 1, pl.ds(first + (tile_rows + 1) * (1 - tile), pieces, stride=stride), :] = row_near[plane]
        far = jnp.where(at_end("tile"), 0.0, row_far[plane])
        pad[plane + 1, pl.ds(first + (tile_rows + 1) * tile, pieces, stride=stride), :] = far


class Marcher:
    def __init__(self, pad, tables_ref, side_ref, stash):
        self.pad, self.stash = pad, stash
        self.pieces = side_ref.shape[1] // LANES
        self.planes = pad.shape[0] - 2
        self.tables = [tables_ref[k] for k in range(tables_ref.shape[0])]
        at = self.tables[0]
        self.edges = [jnp.broadcast_to(at[k : k + 1], (ROWS, LANES)) for k in range(KNOTS)]
        self.lane = lax.broadcasted_iota(jnp.int32, (ROWS, LANES), 1)
        self.lanes = [slice(p * LANES, (p + 1) * LANES) for p in range(self.pieces)]
        self.toward = [jnp.broadcast_to(side_ref[:, c], (ROWS, LANES)) == 1 for c in self.lanes]

    def read(self, group, plane, piece, shift=0):
        row = pad_row(ROWS * ROWS, piece, group + shift)
        return self.pad[plane + 1, pl.ds(row, ROWS, stride=ROWS), :]

    def start(self):
        zero = jnp.zeros((ROWS, LANES), jnp.float32)
        return [[zero] * self.pieces for _ in range(3)] + [[zero + 1.0] * self.pieces]

    def load(self, ref):
        return [[ref[k, :, c] for c in self.lanes] for k in range(4)]

    def store(self, ref, state):
        for k in range(4):
            for p, c in enumerate(self.lanes):
                ref[k, :, c] = state[k][p]

    def shade(self, group, plane, held):
        lane, zero = self.lane, jnp.zeros((ROWS, LANES), jnp.float32)
        for q in range(plane - 1, plane + 2):
            if q not in held:
                held[q] = [self.read(group, q, p) for p in range(self.pieces)]
        before, here, after = [held[plane + d] for d in (-1, 0, 1)]
        to_left = [pltpu.roll(v, LANES - 1, 1) for v in here] + [zero]
        to_right = [zero] + [pltpu.roll(v, 1, 1) for v in here]
        strengths = []
        for p in range(self.pieces):
            depth = after[p] - before[p]
            rows = self.read(group, plane, p, 1) - self.read(group, plane, p, -1)
            col_up = jnp.where(lane == 0, to_right[p], to_right[p + 1])
            col_down = jnp.where(lane == LANES - 1, to_left[p + 1], to_left[p])
            across = col_down - col_up
            facing = jnp.abs(depth + (0.6 / 0.64) * rows + (0.48 / 0.64) * across)
            square = depth * depth + rows * rows + (across * across + 4.0)
            strengths.append(0.3 / FACING + facing * lax.rsqrt(square))
        return here, strengths

    def pair(self, group, plane, held):
        (low, low_strength), (high, high_strength) = [
            self.shade(group, q, held) for q in (plane, self.planes - 1 - plane)
        ]
        near, far = [], []
        for p, toward in enumerate(self.toward):
            near.append((jnp.where(toward, low[p], high[p]), jnp.where(toward, low_strength[p], high_strength[p])))
            far.append((jnp.where(toward, high[p], low[p]), jnp.where(toward, high_strength[p], low_strength[p])))
        return near, far

    def behind(self, state, plane):
        new = [[], [], [], []]
        for p, (x, strength) in enumerate(plane):
            clipped = jnp.minimum(jnp.maximum(x, -3.0), 3.0)
            red, green, blue, exponent = look_up(clipped, self.tables, self.edges)
            left = state[3][p] * jnp.exp2(exponent)
            weight = (state[3][p] - left) * strength
            for channel, value in enumerate((red, green, blue)):
                new[channel].append(state[channel][p] + weight * value)
            new[3].append(left)
        return new

    def run(self, group, first):
        state, held = self.start(), {}
        for plane in range(first, self.planes // 2):
            near, far = self.pair(group, plane, held)
            state = self.behind(state, near)
            for p in range(self.pieces):
                for k in range(2):
                    self.stash[(plane * self.pieces + p) * 2 + k] = far[p][k]
        for plane in reversed(range(first, self.planes // 2)):
            at = [(plane * self.pieces + p) * 2 for p in range(self.pieces)]
            state = self.behind(state, [(self.stash[k], self.stash[k + 1]) for k in at])
        return state

    def ends(self, state, group):
        near, far = self.pair(group, 0, {})
        front = self.behind(self.start(), near)
        state = [
            [front[k][p] + front[3][p] * state[k][p] if k < 3 else front[3][p] * state[3][p] for p in range(self.pieces)]
            for k in range(4)
        ]
        return self.behind(state, far)


def late_group(parity):
    return ROWS - 2 - parity


def inner_kernel(pad, tables_ref, side_ref, states, stash):
    marcher = Marcher(pad, tables_ref, side_ref, stash)
    (core,) = low_bits("slab", 0)

    def group(j, carry):
        g = 1 + j + (1 + j >= late_group(core)).astype(jnp.int32)
        marcher.store(states.at[g], marcher.run(g, 1))
        return carry

    lax.fori_loop(0, ROWS - 3, group, 0, unroll=INNER_UNROLL)


def finish(pad, states, tables_ref, side_ref, out, stash, parity, left):
    marcher = Marcher(pad, tables_ref, side_ref, stash)

    def whole(t, carry):
        g = jnp.where(t == 0, parity * (ROWS - 1), late_group(parity))
        marcher.store(out.at[g >> 1], marcher.run(g, 0))
        return carry

    def group(j, carry):
        g = 2 - parity + 2 * j
        marcher.store(out.at[g >> 1], marcher.ends(marcher.load(states.at[g]), g))
        return carry

    lax.fori_loop(0, left, whole, 0, unroll=True)
    lax.fori_loop(0, ROWS // 2 - left, group, 0, unroll=True)


def merge(first_is_front, mine, other):
    lead = jnp.where(first_is_front, mine[3], other[3])
    merged = [
        jnp.where(first_is_front, mine[c], other[c]) + lead * jnp.where(first_is_front, other[c], mine[c])
        for c in range(3)
    ]
    return merged + [mine[3] * other[3]]


def both_halves(value):
    sublane = lax.broadcasted_iota(jnp.int32, value.shape, 0)
    return jnp.where(sublane < 4, pltpu.roll(value, 4, 0), value)


def final_kernel(parts, side_ref, out):
    ray_order = [k + z for z in range(ROWS) for k in range(0, parts.shape[0], ROWS)]
    toward = jnp.concatenate([side_ref[...]] * 2, axis=0) == 1
    lower = lax.broadcasted_iota(jnp.int32, (ROWS, LANES), 0) < 4
    whole = [(parts[k, :ROWS], parts[k, ROWS:], both_halves(parts[k, ROWS:])) for k in ray_order]
    while len(whole) > 1:
        joined = []
        for (top, bottom, passing), (top_2, bottom_2, passing_2) in zip(whole[::2], whole[1::2]):
            lead = jnp.where(toward, passing, passing_2)
            joined.append((
                jnp.where(toward, top, top_2) + lead * jnp.where(toward, top_2, top),
                jnp.where(toward, bottom, bottom_2) + lead * jnp.where(toward, bottom_2, bottom),
                passing * passing_2,
            ))
        whole = joined
    top, bottom, passing = whole[0]
    out[:ROWS] = top
    out[ROWS:] = jnp.where(lower, bottom, 1.0 - passing)


def per_device(volume, knot_bins, colour_table, view_side):
    planes, tile_rows, columns = volume.shape
    slabs, tiles = lax.axis_size("slab"), lax.axis_size("tile")
    pieces = columns // LANES
    unit = 4 * pieces
    groups = ROWS // 2

    vmem = pl.BlockSpec(memory_space=pltpu.VMEM)
    hbm = pl.BlockSpec(memory_space=pltpu.HBM)
    small = pltpu.CompilerParams(vmem_limit_bytes=SMALL_VMEM)

    def array(*shape):
        return jax.ShapeDtypeStruct(shape, jnp.float32)

    inputs = (volume, knot_bins, colour_table, view_side.reshape(1, columns))
    inputs = [pltpu.with_memory_space_constraint(x, pltpu.HBM) for x in inputs]
    plane = pltpu.VMEM((1, tile_rows, columns), jnp.float32)
    row = pltpu.VMEM((planes, pieces, LANES), jnp.float32)
    pad, *edges, tables, side = pl.pallas_call(
        lambda *refs: load_kernel(planes * slabs, *refs),
        out_shape=[
            pltpu.VMEM((planes + 2, pieces * (tile_rows + 2 * ROWS), LANES), jnp.float32),
            plane, plane, row, row,
            pltpu.VMEM((9, ROWS, LANES), jnp.float32),
            pltpu.VMEM((1, columns), jnp.int32),
        ],
        in_specs=[hbm] * 4,
        out_specs=[vmem] * 7,
        scratch_shapes=[
            pltpu.SMEM((KNOTS,), jnp.int32),
            pltpu.SMEM((4, KNOTS), jnp.float32),
            pltpu.SemaphoreType.DMA((LOAD_PARTS * pieces,)),
            pltpu.SemaphoreType.DMA((3,)),
        ],
        compiler_params=small,
        name="load",
    )(*inputs)

    def swap(block, axis, low):
        route = []
        for slab in range(slabs):
            for tile in range(tiles):
                index, size = (slab, slabs) if axis == "slab" else (tile, tiles)
                step = 1 if (index - low) % 2 == 0 else -1
                if not 0 <= index + step < size:
                    other = (slab, tile ^ 1) if axis == "slab" else (slab ^ 1, tile)
                else:
                    other = (slab + step, tile) if axis == "slab" else (slab, tile + step)
                route.append((slab * tiles + tile, other[0] * tiles + other[1]))
        return lax.ppermute(block, ("slab", "tile"), route)

    halo = [
        swap(edges[0], "slab", 0),
        swap(edges[1], "slab", 1),
        swap(edges[2], "tile", 0),
        swap(edges[3], "tile", 1),
    ]

    def cost(steps):
        count = steps * ROWS * columns
        return pl.CostEstimate(flops=100 * count, bytes_accessed=16 * count, transcendentals=2 * count)

    inner = (ROWS - 3) * (planes - 2)
    outer = (ROWS * planes - inner) // 2
    stash = pltpu.VMEM((planes * pieces, ROWS, LANES), jnp.float32)
    states = pl.pallas_call(
        inner_kernel,
        out_shape=array(ROWS, 4, ROWS, columns),
        in_specs=[vmem] * 3,
        out_specs=vmem,
        scratch_shapes=[stash],
        compiler_params=small,
        cost_estimate=cost(inner),
        name="inner",
    )(pad, tables, side)

    def finish_sent(pad_in, near, far, row_near, row_far, states, tables, side, pad, out, stash):
        add_halo(pad, near, far, row_near, row_far)
        (core,) = low_bits("slab", 0)
        finish(pad, states, tables, side, out, stash, 1 - core, 1)

    def finish_kept(pad, states, tables, side, out, stash):
        (core,) = low_bits("slab", 0)
        finish(pad, states, tables, side, out, stash, core, 2)

    half = array(groups, 4, ROWS, columns)
    pad, sent = pl.pallas_call(
        finish_sent,
        out_shape=[array(*pad.shape), half],
        in_specs=[vmem] * 8,
        out_specs=[vmem] * 2,
        input_output_aliases={0: 0},
        scratch_shapes=[stash],
        compiler_params=small,
        cost_estimate=cost(outer),
        name="finish_sent",
    )(pad, *halo, states, tables, side)
    got = lax.ppermute(sent, "slab", [(i, i ^ 1) for i in range(slabs)])
    kept = pl.pallas_call(
        finish_kept,
        out_shape=half,
        in_specs=[vmem] * 4,
        out_specs=vmem,
        scratch_shapes=[stash],
        compiler_params=small,
        cost_estimate=cost(outer),
        name="finish_kept",
    )(pad, states, tables, side)

    def pair(mine, other, side_ref, out):
        (core,) = low_bits("slab", 0)
        for p in range(pieces):
            c = slice(p * LANES, (p + 1) * LANES)
            front = jnp.broadcast_to(side_ref[:, c], (ROWS, LANES)) + core == 1
            for x in range(groups):
                whole = merge(front, [mine[x, k, :, c] for k in range(4)], [other[x, k, :, c] for k in range(4)])
                for k, value in enumerate(whole):
                    out[pl.ds(x * ROWS * unit + k * pieces + p, ROWS, stride=unit), :] = value

    merged = pl.pallas_call(
        pair,
        out_shape=array(ROWS * groups * unit, LANES),
        in_specs=[vmem] * 3,
        out_specs=vmem,
        compiler_params=small,
        name="pair",
    )(kept, got, side)
    members = [[2 * (z * groups + x) + c for x in range(groups) for z in range(ROWS)] for c in range(2)]
    parts = lax.all_to_all(
        merged.reshape(slabs // 2, unit, LANES), "slab", 0, 0, axis_index_groups=members, tiled=True
    )
    image = pl.pallas_call(
        final_kernel,
        out_shape=array(unit, LANES),
        in_specs=[vmem] * 2,
        out_specs=vmem,
        compiler_params=small,
        name="final",
    )(parts, side.reshape(pieces, LANES))
    return image.reshape(4, 1, 1, columns)


def solution(mesh):
    return jax.shard_map(
        per_device,
        mesh=mesh,
        in_specs=(P("slab", "tile", None), P(), P(), P()),
        out_specs=P(None, "slab", "tile", None),
        check_vma=False,
    )
```
